128 devices in a mesh: ctx: 16 (over x, z_lo, core), dp: 8 (over z_hi, y).
Axes of the slice: x: 4, y: 4, z: 4 (z_hi: 2, z_lo: 2; z = z_hi * 2 + z_lo), core: 2. Of those that a mesh axis runs over, the one named last changes fastest.
Arguments:
- tokens: bfloat16 [1024, 4096], P(('ctx', 'dp')), may hold values from -6 to 6
- cotangent: bfloat16 [1024, 4096], P(('ctx', 'dp')), may hold values from -6 to 6
- expert_ids: int32 [1024, 8], P(('ctx', 'dp')), may hold values from 0 to 63, as said below
- gates: float32 [1024, 8], P(('ctx', 'dp')), may hold values from 0.03 to 0.5
- gate_weight: bfloat16 [128, 4096, 768], P(('ctx', 'dp')), may hold values from -0.09375 to 0.09375
- up_weight: bfloat16 [128, 4096, 768], P(('ctx', 'dp')), may hold values from -0.09375 to 0.09375
- down_weight: bfloat16 [128, 768, 4096], P(('ctx', 'dp')), may hold values from -0.15625 to 0.15625
Outputs:
- mixed: bfloat16 [1024, 4096], P(('ctx', 'dp'))
- gate_grads: float32 [1024, 8], P(('ctx', 'dp'))
- token_grads: bfloat16 [1024, 4096], P(('ctx', 'dp'))
The draws below stay inside these ranges and needn't reach their ends.
Inputs may be any that keep to these rules, and one draw needn't show every extreme that they name: `expert_ids`: each row names 8 different experts. Among the rows of one device each expert is named by either no row or exactly 2 rows, and every expert is named by exactly 2 rows on some device.
All inputs are finite; a program needn't handle non-finite values.
Results may differ from the reference program's by a relative error of at most 0.0065.
Values may be sent and summed in bfloat16 or wider, within the bound.
A program may use at most 128 MiB of HBM per device.

```python
import math
import jax
import jax.numpy as jnp
from jax import lax

D = 4096
FF = 1536
TOPK = 8
HALVES = 2
TOK_DEV = 8
FFH = 768
EXPERTS = 64
CAP = 2
TOKENS = 1024
N_CTX = 16
N_DP = 8


def permute_experts(subkey):
    return jax.random.permutation(subkey, EXPERTS)


def permute_chosen(subkey, chosen):
    return jax.random.permutation(subkey, chosen)


def draw_expert_ids(key, part):
    key = jax.random.fold_in(key, 11)
    blocks_count = TOKENS // TOK_DEV
    pairs_count = blocks_count // 2
    half_count = EXPERTS // 2
    pair_keys = jax.random.split(jax.random.fold_in(key, 1), pairs_count)
    orders = jax.vmap(permute_experts)(pair_keys)
    chosen_sets = orders.reshape(pairs_count * 2, half_count)
    device_keys = jax.random.split(jax.random.fold_in(key, 2), blocks_count)
    shuffled = jax.vmap(permute_chosen)(device_keys, chosen_sets)
    slot_index = jnp.arange(TOK_DEV * TOPK, dtype=jnp.int32) % half_count
    picked_ids = shuffled[:, slot_index]
    return picked_ids.reshape(TOKENS, TOPK).astype(jnp.int32)


def steps_of(key, extent, cuts, low, top_value):
    def one(position, shards_of):
        draws = jax.random.uniform(jax.random.fold_in(jax.random.fold_in(key, 6), position), (shards_of,), jnp.float32, low / len(cuts), top_value / len(cuts))
        return jnp.repeat(jnp.exp(draws), extent[position] // shards_of).reshape((-1,) + (1,) * (len(extent) - position - 1))

    level = one(*cuts[0])
    for cut in cuts[1:]:
        level = level * one(*cut)
    return level


def gaussian(stream_key, extent, spread, reach, pieces=(), kind=jnp.bfloat16):
    values = jax.random.normal(stream_key, extent, jnp.float32) * spread
    if len(pieces) > 0:
        values = steps_of(stream_key, extent, pieces, -0.22, 0.18) * values
    return jnp.clip(values, min=-reach, max=reach).astype(kind)


def setup_inputs(seed: int = 0) -> dict:
    seeds = jax.random.split(jax.random.key(seed), 8)
    tokens = gaussian(seeds[0], (TOKENS, D), 1.0, 6.0, ((0, 128),))
    cotangent = gaussian(seeds[1], (TOKENS, D), 1.0, 6.0, ((0, 128),))
    expert_ids = draw_expert_ids(jax.random.fold_in(seeds[7], 71), 0)
    gates = jnp.clip(jnp.exp(math.log(0.5) - 2.8134107 * jax.random.uniform(seeds[3], (TOKENS, TOPK), jnp.float32) ** steps_of(seeds[3], (TOKENS, TOPK), ((0, 128),), -0.2, 0.2)), 0.03, 0.5)
    gate_weight = gaussian(seeds[4], (EXPERTS * HALVES, D, FFH), D ** -0.5, 0.09375, ((0, 128),))
    up_weight = gaussian(seeds[5], (EXPERTS * HALVES, D, FFH), D ** -0.5, 0.09375, ((0, 128),))
    down_weight = gaussian(seeds[6], (EXPERTS * HALVES, FFH, D), FF ** -0.5, 0.15625, ((0, 128),))
    return {"tokens": tokens, "cotangent": cotangent, "expert_ids": expert_ids, "gates": gates, "gate_weight": gate_weight, "up_weight": up_weight, "down_weight": down_weight}


def half_pass(rows_in, grad_rows, gate_mat, up_mat, down_mat):
    gate_act = jnp.dot(rows_in, gate_mat, preferred_element_type=jnp.float32)
    second = jnp.dot(rows_in, up_mat, preferred_element_type=jnp.float32)
    hidden = (jax.nn.silu(gate_act) * second).astype(jnp.bfloat16)
    partial_value = jnp.dot(hidden, down_mat, preferred_element_type=jnp.float32).astype(jnp.bfloat16)
    backward = jnp.dot(grad_rows, down_mat.T, preferred_element_type=jnp.float32)
    squash = jax.nn.sigmoid(gate_act)
    grad_gate = (backward * second * squash * (1.0 + gate_act * (1.0 - squash))).astype(jnp.bfloat16)
    grad_second = (backward * gate_act * squash).astype(jnp.bfloat16)
    input_part = (jnp.dot(grad_gate, gate_mat.T, preferred_element_type=jnp.float32)
                  + jnp.dot(grad_second, up_mat.T, preferred_element_type=jnp.float32)).astype(jnp.bfloat16)
    return partial_value, input_part


def reference(tokens, cotangent, expert_ids, gates, gate_weight, up_weight, down_weight):
    routes = TOKENS * TOPK
    max_rows = N_CTX * N_DP * CAP
    flat_ids = expert_ids.reshape(-1).astype(jnp.int32)
    by_expert = jnp.argsort(flat_ids, stable=True).astype(jnp.int32)
    counts = jnp.sum((flat_ids[:, None] == jnp.arange(EXPERTS, dtype=jnp.int32)[None, :]).astype(jnp.int32), axis=0)
    starts = (jnp.cumsum(counts) - counts).astype(jnp.int32)
    padded = jnp.concatenate([by_expert, jnp.full((max_rows,), routes, jnp.int32)])

    def one_expert(expert):
        picked = lax.dynamic_slice(padded, (starts[expert],), (max_rows,)).astype(jnp.int32)
        in_use = jnp.arange(max_rows, dtype=jnp.int32) < counts[expert]
        dest_idx = jnp.where(in_use, picked, routes).astype(jnp.int32)
        token_idx = jnp.where(in_use, picked // TOPK, 0).astype(jnp.int32)
        rows_in = jnp.where(in_use[:, None], tokens[token_idx], jnp.zeros_like(tokens[:1]))
        grad_rows = jnp.where(in_use[:, None], cotangent[token_idx], jnp.zeros_like(cotangent[:1]))
        out_sum = jnp.zeros((max_rows, D), jnp.float32)
        grad_sum = jnp.zeros((max_rows, D), jnp.float32)
        for half_idx in range(HALVES):
            weight_row = expert * HALVES + half_idx
            partial_value, input_part = half_pass(rows_in, grad_rows, gate_weight[weight_row], up_weight[weight_row], down_weight[weight_row])
            out_sum = out_sum + partial_value.astype(jnp.float32)
            grad_sum = grad_sum + input_part.astype(jnp.float32)
        return out_sum.astype(jnp.bfloat16), grad_sum.astype(jnp.bfloat16), dest_idx

    outputs, in_grads, dest_all = lax.map(one_expert, jnp.arange(EXPERTS, dtype=jnp.int32))
    dest_flat = dest_all.reshape(-1)
    expert_out = jnp.zeros((routes, D), jnp.bfloat16).at[dest_flat].set(outputs.reshape(-1, D), mode="drop")
    route_grad = jnp.zeros((routes, D), jnp.bfloat16).at[dest_flat].set(in_grads.reshape(-1, D), mode="drop")
    routed = expert_out.reshape(TOKENS, TOPK, D).astype(jnp.float32)
    routed_grad = route_grad.reshape(TOKENS, TOPK, D).astype(jnp.float32)
    mixed = jnp.sum(gates[:, :, None] * routed, axis=1).astype(jnp.bfloat16)
    gate_grads = jnp.sum(cotangent.astype(jnp.float32)[:, None, :] * routed, axis=2)
    token_grads = jnp.sum(gates[:, :, None] * routed_grad, axis=1).astype(jnp.bfloat16)
    return (mixed, gate_grads, token_grads)
```

```python
import functools

import jax
import jax.numpy as jnp
from jax import lax
from jax.experimental import pallas as pl
from jax.experimental.pallas import tpu as pltpu
from jax.sharding import PartitionSpec as P

MESH = pl.DeviceIdType.MESH
BF16 = jnp.bfloat16
F32 = jnp.float32
LANES = 128
RING = 4
EXPERTS = 64
SLOTS = 256
HIDDEN = 768
WIDTH = 4096

ORDERS = ((2, 1, 0), (0, 2, 1), (1, 0, 2))
STARTS = (0, 1408, 2816)
WIDTHS = (1408, 1408, 1280)
MASKED = (1536, 1536, 1536)
CARRIED = (1408, 1408, 1408)
PARTS = range(3)


def device_at(place, core):
    x, y, z = place
    return (x * 4 + (z % 2) * 2 + core, (z // 2) * 4 + y)


def expert_at(place, core):
    x, y, z = place
    return x * 16 + (z % 2) * 8 + core * 4 + (z // 2) * 2 + y // 2


def moved(place, axis, value):
    return tuple(value if i == axis else place[i] for i in range(3))


def iota(shape, axis):
    return lax.broadcasted_iota(jnp.int32, shape, axis)


def dot(a, b):
    return jnp.dot(a, b, preferred_element_type=F32)


def dot_nt(a, b):
    return lax.dot_general(a, b, (((1,), (1,)), ((), ())), preferred_element_type=F32)


def blocks(width, size):
    return [(i, min(size, width - i)) for i in range(0, width, size)]


def slot_coordinates(index, part):
    first, middle, last = ORDERS[part]
    coords = [None] * 3
    coords[last] = index // 64
    coords[middle] = (index // 8) % 4
    coords[first] = (index // 2) % 4
    return coords, (index // 32) % 2, index % 2


def index_in(part, coords, core, slot):
    first, middle, last = ORDERS[part]
    return coords[last] * 64 + core * 32 + coords[middle] * 8 + coords[first] * 2 + slot


def reorder(part, back):
    rows, cols = iota((SLOTS, SLOTS), 0), iota((SLOTS, SLOTS), 1)
    mine, other = (cols, rows) if back else (rows, cols)
    coords, core, slot = slot_coordinates(mine, part)
    return (index_in(0, coords, core, slot) == other).astype(F32).astype(BF16)


def kernel(
    tokens_ref, cotangent_ref, ids_ref, gates_ref, gate_hbm, up_hbm, down_hbm,
    mixed_ref, gate_grads_ref, token_grads_ref,
    gate_w, up_w, down_w,
    gathered, token_send, token_recv, grad_send, grad_recv,
    act, out_send, out_recv, in_send, in_recv,
    out_mid, out_mid_recv, in_mid, in_mid_recv, end_send, end_recv,
    out_sum,
    weight_sem, local_sem,
    s1_send, s1_recv, s2_send, s2_recv, t3_send, t3_recv, c3_send, c3_recv,
    m3_send, m3_recv, g3_send, g3_recv, m2_send, m2_recv, g2_send, g2_recv, e1_send, e1_recv,
):
    ctx, dp = lax.axis_index("ctx"), lax.axis_index("dp")
    place = (ctx // 4, dp % 4, (dp // 4) * 2 + (ctx // 2) % 2)
    core = ctx % 2
    expert = expert_at(place, core)

    barrier = pltpu.get_barrier_semaphore()
    peers = [(place, 1 - core)]
    for axis in range(3):
        for offset in range(1, RING):
            there = moved(place, axis, (place[axis] + offset) % RING)
            peers += [(there, core), (there, 1 - core)]
    for there, its_core in peers:
        pl.semaphore_signal(
            barrier, inc=1, device_id=device_at(there, its_core), device_id_type=MESH
        )

    loads = [
        pltpu.make_async_copy(src.at[0], dst, weight_sem.at[i])
        for i, (src, dst) in enumerate(((gate_hbm, gate_w), (up_hbm, up_w), (down_hbm, down_w)))
    ]
    for load in loads:
        load.start()

    lane = iota((8, LANES), 1)
    named = jnp.zeros((8, LANES), F32)
    gate = jnp.zeros((8, LANES), F32)
    for k in range(8):
        hit = ids_ref[:, k : k + 1] == lane % EXPERTS
        named = jnp.where(hit, 1.0, named)
        gate = jnp.where(hit, gates_ref[:, k : k + 1], gate)
    row = iota((8, LANES), 0)
    before = jnp.zeros((8, LANES), F32)
    for i in range(7):
        before = before + jnp.where(row > i, named[i : i + 1, :], 0.0)
    slots = jnp.where(before == (lane // EXPERTS).astype(F32), named, 0.0)
    gate_high = gate.astype(BF16).astype(F32)
    gate_tile = jnp.where(lane < EXPERTS, gate_high, gate - gate_high)

    def both(top, bottom):
        return jnp.concatenate((top, bottom), axis=0).astype(BF16)

    for p in PARTS:
        first, middle, last = ORDERS[p]
        home = gathered[p].at[place[middle], place[first]]
        cols = pl.ds(STARTS[p], WIDTHS[p])
        home[:, pl.ds(0, WIDTHS[p])] = both(
            tokens_ref[:, cols].astype(F32), cotangent_ref[:, cols].astype(F32)
        )
        if p == 2:
            home[:, pl.ds(WIDTHS[p], LANES)] = both(gate_tile, jnp.zeros_like(gate_tile))
        home[:, pl.ds(CARRIED[p], LANES)] = both(slots, slots)

    pl.semaphore_wait(barrier, len(peers))

    pending = []

    def ring(axis, p, source, target, send_sem, recv_sem):
        copies = []
        for offset in range(1, RING):
            there = moved(place, axis, (place[axis] + offset) % RING)
            copy = pltpu.make_async_remote_copy(
                src_ref=source(there[axis]),
                dst_ref=target(offset),
                send_sem=send_sem.at[p, offset - 1],
                recv_sem=recv_sem.at[p, offset - 1],
                device_id=device_at(there, core),
                device_id_type=MESH,
            )
            copy.start()
            copies.append(copy)
        pending.extend(copies)
        return copies

    def exchange(axis, p, source, target, send_sem, recv_sem, kind):
        copies = []
        for offset in range(RING):
            there = moved(place, axis, (place[axis] + offset) % RING)
            for flip in range(2):
                its_core = core if flip == 0 else 1 - core
                src = source.at[there[axis], its_core]
                dst = target.at[place[axis], core]
                if offset == 0 and flip == 0:
                    continue
                copy = pltpu.make_async_remote_copy(
                    src_ref=src,
                    dst_ref=dst,
                    send_sem=send_sem.at[p, offset * 2 + flip - 1],
                    recv_sem=recv_sem.at[p, offset * 2 + flip - 1],
                    device_id=device_at(there, its_core),
                    device_id_type=MESH,
                )
                copy.start()
                copies.append(copy)
        own = pltpu.make_async_copy(
            source.at[place[axis], core], target.at[place[axis], core], local_sem.at[kind, p]
        )
        own.start()
        pending.extend(copies)
        return copies, own

    def arrived(copies):
        for copy in copies:
            copy.wait_recv()

    def exchanged(copies):
        arrived(copies[0])
        copies[1].wait()

    stage = []
    for p in PARTS:
        first, middle, last = ORDERS[p]
        home = gathered[p].at[place[middle], place[first]]
        stage.append(
            ring(first, p, lambda there: home, lambda offset: home, s1_send, s1_recv)
        )
    stage2 = []
    for p in PARTS:
        first, middle, last = ORDERS[p]
        home = gathered[p].at[place[middle]]
        arrived(stage[p])
        stage2.append(
            ring(middle, p, lambda there: home, lambda offset: home, s2_send, s2_recv)
        )

    r0, r1 = iota((SLOTS, SLOTS), 0), iota((SLOTS, SLOTS), 1)
    same = (r0 // 2) % 16 == r1 // 16
    top = same & ((r1 // 8) % 2 == 0)
    low = same & ((r1 // 8) % 2 == 1)
    u0, u1 = iota((SLOTS // 2, SLOTS), 0), iota((SLOTS // 2, SLOTS), 1)
    same_back = u0 // 8 == (u1 // 2) % 16
    lane = iota((SLOTS, LANES), 1)
    to_home = []
    token_copies, grad_copies, low_masks = [], [], []
    for p in PARTS:
        first, middle, last = ORDERS[p]
        arrived(stage2[p])
        index = iota((SLOTS, LANES), 0)
        wanted = expert_at(moved(place, last, index // 64), (index // 32) % 2)
        pick = (lane == (index % 2) * EXPERTS + wanted).astype(F32).astype(BF16)
        tile = gathered[p][:, :, :, CARRIED[p] : CARRIED[p] + LANES].reshape(SLOTS, LANES)
        chosen = dot_nt(pick, tile)
        from_tokens = jnp.where(top, chosen, 0.0).astype(BF16)
        low_masks.append(jnp.where(low, chosen, 0.0).astype(BF16))
        half = tile.astype(F32).reshape(16, 2, 8, LANES)[:, 0].reshape(SLOTS // 2, LANES)
        to_home.append(jnp.where(same_back, dot_nt(half.astype(BF16), pick), 0.0).astype(BF16))
        for start, size in blocks(CARRIED[p], 256):
            rows = gathered[p][:, :, :, start : start + size].reshape(SLOTS, size)
            token_send[p][:, :, :, start : start + size] = (
                dot(from_tokens, rows).astype(BF16).reshape(RING, 2, 32, size)
            )
        token_copies.append(
            exchange(last, p, token_send[p], token_recv[p], t3_send, t3_recv, 0)
        )
    for p in PARTS:
        last = ORDERS[p][2]
        for start, size in blocks(WIDTHS[p], 256):
            rows = gathered[p][:, :, :, start : start + size].reshape(SLOTS, size)
            grad_send[p][:, :, :, start : start + size] = (
                dot(low_masks[p], rows).astype(BF16).reshape(RING, 2, 32, size)
            )
        grad_copies.append(exchange(last, p, grad_send[p], grad_recv[p], c3_send, c3_recv, 1))

    def in_order(p, recv, width):
        rows = recv[p][:, :, :, 0:width].reshape(SLOTS, width)
        if p == 0:
            return rows
        return dot(reorder(p, True), rows).astype(BF16)

    gate_slot = None
    loads[0].wait()
    loads[1].wait()
    for p in PARTS:
        exchanged(token_copies[p])
        rows = in_order(p, token_recv, CARRIED[p])
        if p == 2:
            tile = rows[:, WIDTHS[p] :].astype(F32)
            gate_slot = jnp.sum(
                jnp.where(lane % EXPERTS == expert, tile, 0.0), axis=1, keepdims=True
            )
            rows = rows[:, : WIDTHS[p]]
        feats = slice(STARTS[p], STARTS[p] + WIDTHS[p])
        for half_i, weight in enumerate((gate_w, up_w)):
            for start, size in blocks(HIDDEN, 256):
                value = dot(rows, weight[feats, start : start + size])
                if p == 0:
                    act[half_i, :, start : start + size] = value
                else:
                    act[half_i, :, start : start + size] += value
    gate_act, second = act[0], act[1]
    squash = jax.nn.sigmoid(gate_act)
    hidden = gate_act * squash * second
    hidden_gated = (gate_slot * hidden).astype(BF16)
    act[2] = hidden
    loads[2].wait()

    def sent_order(p, value):
        if p == 0:
            return value
        return dot(reorder(p, False), value).astype(BF16)

    out_copies = []
    for p in PARTS:
        rows = sent_order(p, hidden_gated)
        for start, size in blocks(WIDTHS[p], 256):
            at = STARTS[p] + start
            out_send[p][:, :, :, start : start + size] = (
                dot(rows, down_w[:, at : at + size]).astype(BF16).reshape(RING, 2, 32, size)
            )
        out_copies.append(
            exchange(ORDERS[p][2], p, out_send[p], out_recv[p], m3_send, m3_recv, 2)
        )

    backward = [None] * 3
    for p in PARTS:
        exchanged(grad_copies[p])
        rows = in_order(p, grad_recv, WIDTHS[p])
        feats = slice(STARTS[p], STARTS[p] + WIDTHS[p])
        for i, (start, size) in enumerate(blocks(HIDDEN, 256)):
            value = dot_nt(rows, down_w[start : start + size, feats])
            if p == 0:
                act[3, :, start : start + size] = value
            else:
                act[3, :, start : start + size] += value
    backward = act[3]
    gate_act, second = act[0], act[1]
    squash = jax.nn.sigmoid(gate_act)
    gate_grad = jnp.sum(backward * act[2], axis=1, keepdims=True)
    scaled = backward * gate_slot * squash
    grad_gate = (scaled * second * (1.0 + gate_act * (1.0 - squash))).astype(BF16)
    grad_second = (scaled * gate_act).astype(BF16)
    grad_high = gate_grad.astype(BF16).astype(F32)
    grad_tile = jnp.where(
        lane == expert, grad_high, jnp.where(lane == expert + EXPERTS, gate_grad - grad_high, 0.0)
    ).astype(BF16)

    in_copies = []
    for p in PARTS:
        rows_gate = sent_order(p, grad_gate)
        rows_second = sent_order(p, grad_second)
        for start, size in blocks(WIDTHS[p], 256):
            at = STARTS[p] + start
            value = dot_nt(rows_gate, gate_w[at : at + size, :]) + dot_nt(
                rows_second, up_w[at : at + size, :]
            )
            in_send[p][:, :, :, start : start + size] = value.astype(BF16).reshape(
                RING, 2, 32, size
            )
        if p == 2:
            in_send[p][:, :, :, WIDTHS[p] :] = sent_order(p, grad_tile).reshape(
                RING, 2, 32, LANES
            )
        in_copies.append(exchange(ORDERS[p][2], p, in_send[p], in_recv[p], g3_send, g3_recv, 3))

    def to_middle(p, copies, recv, mid, mid_recv, width, send_sem, recv_sem):
        exchanged(copies[p])
        for start, size in blocks(width, 256):
            rows = recv[p][:, :, :, start : start + size].reshape(SLOTS, size)
            mid[p][:, :, start : start + size] = (
                dot(to_home[p], rows).astype(BF16).reshape(RING, 32, size)
            )
        return ring(
            ORDERS[p][1], p, lambda there: mid[p].at[there],
            lambda offset: mid_recv[p].at[offset - 1], send_sem, recv_sem,
        )

    def middle_sum(p, copies, mid, mid_recv):
        arrived(copies[p])
        value = mid[p].at[place[ORDERS[p][1]]][...].astype(F32)
        for i in range(3):
            value = value + mid_recv[p][i].astype(F32)
        return value

    out_mids = [
        to_middle(p, out_copies, out_recv, out_mid, out_mid_recv, WIDTHS[p], m2_send, m2_recv)
        for p in PARTS
    ]
    for p in PARTS:
        out_sum[p][...] = middle_sum(p, out_mids, out_mid, out_mid_recv)
    in_mids = [
        to_middle(p, in_copies, in_recv, in_mid, in_mid_recv, CARRIED[p], g2_send, g2_recv)
        for p in PARTS
    ]
    ends = []
    for p in PARTS:
        outs = out_sum[p][...].reshape(RING, 8, WIDTHS[p])
        ins = middle_sum(p, in_mids, in_mid, in_mid_recv).reshape(RING, 8, CARRIED[p])
        end_send[p][:, :, : WIDTHS[p]] = jnp.concatenate(
            (outs, ins[:, :, : WIDTHS[p]]), axis=1
        ).astype(BF16)
        if p == 2:
            tail = ins[:, :, WIDTHS[p] :]
            end_send[p][:, :, WIDTHS[p] :] = jnp.concatenate((tail, tail), axis=1).astype(BF16)
        ends.append(
            ring(
                ORDERS[p][0], p, lambda there: end_send[p].at[there],
                lambda offset: end_recv[p].at[offset - 1], e1_send, e1_recv,
            )
        )
    for p in PARTS:
        arrived(ends[p])
        value = end_send[p].at[place[ORDERS[p][0]]][...].astype(F32)
        for i in range(3):
            value = value + end_recv[p][i].astype(F32)
        cols = slice(STARTS[p], STARTS[p] + WIDTHS[p])
        mixed_ref[:, cols] = value[:8, : WIDTHS[p]].astype(BF16)
        token_grads_ref[:, cols] = value[8:, : WIDTHS[p]].astype(BF16)
        if p == 2:
            tile = value[8:, WIDTHS[p] :]
            lane8 = iota((8, LANES), 1)
            picked = []
            for k in range(8):
                hit = ids_ref[:, k : k + 1] == lane8 % EXPERTS
                picked.append(jnp.sum(jnp.where(hit, tile, 0.0), axis=1, keepdims=True))
            column = iota((8, 8), 1)
            grads = jnp.zeros((8, 8), F32)
            for k in range(8):
                grads = jnp.where(column == k, picked[k], grads)
            gate_grads_ref[...] = grads

    for copy in pending:
        copy.wait_send()


def shards(tokens, cotangent, expert_ids, gates, gate_weight, up_weight, down_weight):
    def vmem(shape, dtype=BF16):
        return pltpu.VMEM(shape, dtype)

    def parts(shape, widths, dtype=BF16):
        return [vmem((*shape, width), dtype) for width in widths]

    dma = pltpu.SemaphoreType.DMA
    block = (RING, 2, 32)
    whole = pl.BlockSpec(memory_space=pltpu.VMEM)
    hbm = pl.BlockSpec(memory_space=pl.ANY)
    return pl.pallas_call(
        kernel,
        out_shape=(
            jax.ShapeDtypeStruct((8, WIDTH), BF16),
            jax.ShapeDtypeStruct((8, 8), F32),
            jax.ShapeDtypeStruct((8, WIDTH), BF16),
        ),
        in_specs=[whole] * 4 + [hbm] * 3,
        out_specs=[whole] * 3,
        scratch_shapes=[
            vmem((WIDTH, HIDDEN)),
            vmem((WIDTH, HIDDEN)),
            vmem((HIDDEN, WIDTH)),
            parts((RING, RING, 16), MASKED),
            parts(block, CARRIED),
            parts(block, CARRIED),
            parts(block, WIDTHS),
            parts(block, WIDTHS),
            vmem((4, SLOTS, HIDDEN), F32),
            parts(block, WIDTHS),
            parts(block, WIDTHS),
            parts(block, CARRIED),
            parts(block, CARRIED),
            parts((RING, 32), WIDTHS),
            parts((RING - 1, 32), WIDTHS),
            parts((RING, 32), CARRIED),
            parts((RING - 1, 32), CARRIED),
            parts((RING, 16), CARRIED),
            parts((RING - 1, 16), CARRIED),
            parts((32,), WIDTHS, F32),
            dma((3,)),
            dma((4, 3)),
            dma((3, 3)), dma((3, 3)), dma((3, 3)), dma((3, 3)),
            dma((3, 7)), dma((3, 7)), dma((3, 7)), dma((3, 7)),
            dma((3, 7)), dma((3, 7)), dma((3, 7)), dma((3, 7)),
            dma((3, 3)), dma((3, 3)), dma((3, 3)), dma((3, 3)),
            dma((3, 3)), dma((3, 3)),
        ],
        compiler_params=pltpu.CompilerParams(
            collective_id=0, has_side_effects=True, vmem_limit_bytes=60 * 2**20
        ),
    )(tokens, cotangent, expert_ids, gates, gate_weight, up_weight, down_weight)


def solution(mesh):
    rows = P(("ctx", "dp"), None)
    weights = P(("ctx", "dp"), None, None)
    return jax.shard_map(
        shards,
        mesh=mesh,
        in_specs=(rows, rows, rows, rows, weights, weights, weights),
        out_specs=(rows, rows, rows),
        check_vma=False,
    )
```

```python
import functools

import jax
import jax.numpy as jnp
from jax import lax
from jax.experimental import pallas as pl
from jax.experimental.pallas import tpu as pltpu
from jax.sharding import PartitionSpec as P

MESH = pl.DeviceIdType.MESH
BF16 = jnp.bfloat16
F32 = jnp.float32
LANES = 128
RING = 4
EXPERTS = 64
SLOTS = 256
HIDDEN = 768
WIDTH = 4096

ORDERS = ((2, 1, 0), (0, 2, 1), (1, 0, 2))
STARTS = (0, 1408, 2816)
WIDTHS = (1408, 1408, 1280)
TOP = 768
LOWS = (640, 640, 512)
LOW = 640
CARRIED = TOP + LOW
PARTS = range(3)


def device_at(place, core):
    x, y, z = place
    return (x * 4 + (z % 2) * 2 + core, (z // 2) * 4 + y)


def expert_at(place, core):
    x, y, z = place
    return x * 16 + (z % 2) * 8 + core * 4 + (z // 2) * 2 + y // 2


def moved(place, axis, value):
    return tuple(value if i == axis else place[i] for i in range(3))


def iota(shape, axis):
    return lax.broadcasted_iota(jnp.int32, shape, axis)


def dot(a, b):
    return jnp.dot(a, b, preferred_element_type=F32)


def dot_nt(a, b):
    return lax.dot_general(a, b, (((1,), (1,)), ((), ())), preferred_element_type=F32)


def blocks(width, size):
    return [(i, min(size, width - i)) for i in range(0, width, size)]


def slot_coordinates(index, part):
    first, middle, last = ORDERS[part]
    coords = [None] * 3
    coords[last] = index // 64
    coords[middle] = (index // 8) % 4
    coords[first] = (index // 2) % 4
    return coords, (index // 32) % 2, index % 2


def index_in(part, coords, core, slot):
    first, middle, last = ORDERS[part]
    return coords[last] * 64 + core * 32 + coords[middle] * 8 + coords[first] * 2 + slot


def reorder(part, back):
    rows, cols = iota((SLOTS, SLOTS), 0), iota((SLOTS, SLOTS), 1)
    mine, other = (cols, rows) if back else (rows, cols)
    coords, core, slot = slot_coordinates(mine, part)
    return (index_in(0, coords, core, slot) == other).astype(F32).astype(BF16)


def kernel(
    tokens_hbm, cotangent_hbm, ids_hbm, gates_hbm, gate_hbm, up_hbm, down_hbm,
    mixed_ref, gate_grads_ref, token_grads_ref,
    tokens_ref, cotangent_ref, ids_ref, gates_ref, gate_w, up_w, down_w,
    token_rows, grad_rows, token_send, token_recv, grad_send, grad_recv,
    act, out_send, out_recv, in_send, in_recv,
    out_mid, out_mid_recv, in_mid, in_mid_recv, end_send, end_recv,
    input_sem, weight_sem,
    s1_send, s1_recv, s2_send, s2_recv, t3_send, t3_recv, c3_send, c3_recv,
    m3_send, m3_recv, g3_send, g3_recv, m2_send, m2_recv, g2_send, g2_recv, e1_send, e1_recv,
):
    ctx, dp = lax.axis_index("ctx"), lax.axis_index("dp")
    place = (ctx // 4, dp % 4, (dp // 4) * 2 + (ctx // 2) % 2)
    core = ctx % 2
    expert = expert_at(place, core)

    barrier = pltpu.get_barrier_semaphore()
    peers = [(place, 1 - core)]
    for axis in range(3):
        for offset in range(1, RING):
            there = moved(place, axis, (place[axis] + offset) % RING)
            peers += [(there, core), (there, 1 - core)]
    for there, its_core in peers:
        pl.semaphore_signal(
            barrier, inc=1, device_id=device_at(there, its_core), device_id_type=MESH
        )

    inputs = [
        pltpu.make_async_copy(src, dst, input_sem.at[i])
        for i, (src, dst) in enumerate(
            (
                (ids_hbm, ids_ref),
                (gates_hbm, gates_ref),
                (tokens_hbm, tokens_ref),
                (cotangent_hbm, cotangent_ref),
            )
        )
    ]
    for load in inputs:
        load.start()
    loads = [
        pltpu.make_async_copy(src.at[0], dst, weight_sem.at[i])
        for i, (src, dst) in enumerate(((gate_hbm, gate_w), (up_hbm, up_w), (down_hbm, down_w)))
    ]

    inputs[0].wait()
    inputs[1].wait()
    lane = iota((8, LANES), 1)
    named = jnp.zeros((8, LANES), F32)
    gate = jnp.zeros((8, LANES), F32)
    for k in range(8):
        hit = ids_ref[:, k : k + 1] == lane % EXPERTS
        named = jnp.where(hit, 1.0, named)
        gate = jnp.where(hit, gates_ref[:, k : k + 1], gate)
    row = iota((8, LANES), 0)
    before = jnp.zeros((8, LANES), F32)
    for i in range(7):
        before = before + jnp.where(row > i, named[i : i + 1, :], 0.0)
    slots = jnp.where(before == (lane // EXPERTS).astype(F32), named, 0.0)
    gate_high = gate.astype(BF16).astype(F32)
    gate_tile = jnp.where(lane < EXPERTS, gate_high, gate - gate_high)

    def stacked(ref, p, tiles):
        cut = STARTS[p] + TOP
        top = ref[:, STARTS[p] : cut].astype(F32)
        low = ref[:, cut : cut + LOWS[p]].astype(F32)
        return jnp.concatenate((top, jnp.concatenate((low, *tiles), axis=1)), axis=0).astype(BF16)

    inputs[2].wait()
    for p in PARTS:
        first, middle, last = ORDERS[p]
        tiles = (gate_tile, slots) if p == 2 else (slots,)
        token_rows[p, place[middle], place[first]] = stacked(tokens_ref, p, tiles)
    inputs[3].wait()
    for p in PARTS:
        first, middle, last = ORDERS[p]
        blank = jnp.zeros((8, TOP - LOWS[p]), F32)
        grad_rows[p, place[middle], place[first]] = stacked(cotangent_ref, p, (blank,))

    pl.semaphore_wait(barrier, len(peers))

    def taken(ref, sem):
        pltpu.make_async_copy(ref, ref, sem).wait()

    def ring(axis, source, target, send_sem, recv_sem):
        for offset in range(1, RING):
            there = moved(place, axis, (place[axis] + offset) % RING)
            pltpu.make_async_remote_copy(
                src_ref=source(there[axis]),
                dst_ref=target(offset),
                send_sem=send_sem,
                recv_sem=recv_sem,
                device_id=device_at(there, core),
                device_id_type=MESH,
            ).start()

    def exchange(axis, source, target, send_sem, recv_sem):
        mine = target.at[2 * place[axis] + core]
        for offset in (2, 1, 3, 0):
            there = moved(place, axis, (place[axis] + offset) % RING)
            for flip in range(2):
                its_core = core if flip == 0 else 1 - core
                block = source.at[2 * there[axis] + its_core]
                if offset == 0 and flip == 0:
                    pltpu.make_async_copy(block, mine, recv_sem).start()
                    continue
                pltpu.make_async_remote_copy(
                    src_ref=block,
                    dst_ref=mine,
                    send_sem=send_sem,
                    recv_sem=recv_sem,
                    device_id=device_at(there, its_core),
                    device_id_type=MESH,
                ).start()

    kinds = (token_rows, grad_rows)
    for kind, rows in enumerate(kinds):
        for p in PARTS:
            first, middle, last = ORDERS[p]
            home = rows.at[p, place[middle], place[first]]
            ring(
                first, lambda there: home, lambda offset: home,
                s1_send.at[kind], s1_recv.at[kind, p],
            )
    for load in loads:
        load.start()
    for kind, rows in enumerate(kinds):
        for p in PARTS:
            first, middle, last = ORDERS[p]
            home = rows.at[p, place[middle]]
            taken(rows.at[p, 0, pl.ds(0, 3)], s1_recv.at[kind, p])
            ring(
                middle, lambda there: home, lambda offset: home,
                s2_send.at[kind], s2_recv.at[kind, p],
            )

    r0, r1 = iota((SLOTS, SLOTS), 0), iota((SLOTS, SLOTS), 1)
    same = (r0 // 2) % 16 == r1 // 16
    half_masks = [same & ((r1 // 8) % 2 == h) for h in range(2)]
    u0, u1 = iota((SLOTS // 2, SLOTS), 0), iota((SLOTS // 2, SLOTS), 1)
    same_back = u0 // 8 == (u1 // 2) % 16
    lane = iota((SLOTS, LANES), 1)
    to_home, picks = [], []

    def pick_rows(p, h, rows, out, base, width):
        for start, size in blocks(width, 256):
            part = rows[p, :, :, :, start : start + size].reshape(SLOTS, size)
            out[:, :, base + start : base + start + size] = (
                dot(picks[p][h], part).astype(BF16).reshape(8, 32, size)
            )

    for p in PARTS:
        first, middle, last = ORDERS[p]
        taken(token_rows.at[p, pl.ds(0, 3)], s2_recv.at[0, p])
        index = iota((SLOTS, LANES), 0)
        wanted = expert_at(moved(place, last, index // 64), (index // 32) % 2)
        pick = (lane == (index % 2) * EXPERTS + wanted).astype(F32).astype(BF16)
        tile = token_rows[p, :, :, :, LOW:TOP].reshape(SLOTS, LANES)
        tile = tile.astype(F32).reshape(16, 2, 8, LANES)[:, 1]
        twice = jnp.concatenate((tile, tile), axis=1).reshape(SLOTS, LANES).astype(BF16)
        chosen = dot_nt(pick, twice)
        picks.append([jnp.where(mask, chosen, 0.0).astype(BF16) for mask in half_masks])
        home = dot_nt(tile.reshape(SLOTS // 2, LANES).astype(BF16), pick)
        to_home.append(jnp.where(same_back, home, 0.0).astype(BF16))
        pick_rows(p, 0, token_rows, token_send[0].at[p], 0, TOP)
        exchange(
            last, token_send[0].at[p], token_recv[0].at[p], t3_send.at[0], t3_recv.at[0, p]
        )
    for p in PARTS:
        pick_rows(p, 1, token_rows, token_send[1].at[p], 0, LOW)
        exchange(
            ORDERS[p][2], token_send[1].at[p], token_recv[1].at[p],
            t3_send.at[1], t3_recv.at[1, p],
        )
    for p in PARTS:
        taken(grad_rows.at[p, pl.ds(0, 3)], s2_recv.at[1, p])
        pick_rows(p, 0, grad_rows, grad_send.at[p], 0, TOP)
        pick_rows(p, 1, grad_rows, grad_send.at[p], TOP, LOW)
        exchange(
            ORDERS[p][2], grad_send.at[p], grad_recv.at[p], c3_send.at[0], c3_recv.at[p]
        )

    def in_order(p, rows):
        return rows if p == 0 else dot(reorder(p, True), rows).astype(BF16)

    gate_slot = None
    loads[0].wait()
    loads[1].wait()
    for h in range(2):
        for p in PARTS:
            taken(token_recv[h].at[p], t3_recv.at[h, p])
            rows = in_order(p, token_recv[h][p].reshape(SLOTS, (TOP, LOW)[h]))
            size = (TOP, LOWS[p])[h]
            if h == 1 and p == 2:
                tile = rows[:, size:].astype(F32)
                gate_slot = jnp.sum(
                    jnp.where(lane % EXPERTS == expert, tile, 0.0), axis=1, keepdims=True
                )
                rows = rows[:, :size]
            begin = STARTS[p] + h * TOP
            for i, weight in enumerate((gate_w, up_w)):
                for start, width in blocks(HIDDEN, 256):
                    value = dot(rows, weight[begin : begin + size, start : start + width])
                    if h == 0 and p == 0:
                        act[i, :, start : start + width] = value
                    else:
                        act[i, :, start : start + width] += value
    gate_act, second = act[0], act[1]
    squash = jax.nn.sigmoid(gate_act)
    hidden = gate_act * squash * second
    hidden_gated = (gate_slot * hidden).astype(BF16)
    act[2] = hidden
    loads[2].wait()

    def sent_order(p, value):
        return value if p == 0 else dot(reorder(p, False), value).astype(BF16)

    for p in PARTS:
        rows = sent_order(p, hidden_gated)
        for start, size in blocks(WIDTHS[p], 256):
            at = STARTS[p] + start
            out_send[p, :, :, start : start + size] = (
                dot(rows, down_w[:, at : at + size]).astype(BF16).reshape(8, 32, size)
            )
        if p == 2:
            out_send[p, :, :, WIDTHS[p] :] = jnp.zeros((8, 32, LANES), BF16)
        exchange(ORDERS[p][2], out_send.at[p], out_recv.at[p], m3_send.at[0], m3_recv.at[p])

    for p in PARTS:
        taken(grad_recv.at[p], c3_recv.at[p])
        rows = in_order(p, grad_recv[p, :, :, : WIDTHS[p]].reshape(SLOTS, WIDTHS[p]))
        feats = slice(STARTS[p], STARTS[p] + WIDTHS[p])
        for start, size in blocks(HIDDEN, 256):
            value = dot_nt(rows, down_w[start : start + size, feats])
            if p == 0:
                act[3, :, start : start + size] = value
            else:
                act[3, :, start : start + size] += value
    backward = act[3]
    gate_act, second = act[0], act[1]
    squash = jax.nn.sigmoid(gate_act)
    gate_grad = jnp.sum(backward * act[2], axis=1, keepdims=True)
    scaled = backward * gate_slot * squash
    grad_gate = (scaled * second * (1.0 + gate_act * (1.0 - squash))).astype(BF16)
    grad_second = (scaled * gate_act).astype(BF16)
    grad_high = gate_grad.astype(BF16).astype(F32)
    grad_tile = jnp.where(
        lane == expert, grad_high, jnp.where(lane == expert + EXPERTS, gate_grad - grad_high, 0.0)
    ).astype(BF16)
    sent_gate = [sent_order(p, grad_gate) for p in PARTS]
    sent_second = [sent_order(p, grad_second) for p in PARTS]

    def send_gradients(h):
        for p in PARTS:
            width = (TOP, LOWS[p])[h]
            for start, size in blocks(width, 256):
                at = STARTS[p] + h * TOP + start
                value = dot_nt(sent_gate[p], gate_w[at : at + size, :]) + dot_nt(
                    sent_second[p], up_w[at : at + size, :]
                )
                in_send[h][p, :, :, start : start + size] = value.astype(BF16).reshape(8, 32, size)
            if h == 1 and p == 2:
                in_send[h][p, :, :, width:] = sent_order(p, grad_tile).reshape(8, 32, LANES)
            exchange(
                ORDERS[p][2], in_send[h].at[p], in_recv[h].at[p],
                g3_send.at[h], g3_recv.at[h, p],
            )

    def to_middle(p, recv, mid, mid_recv, width, sem, send_sem, recv_sem):
        taken(recv, sem)
        for start, size in blocks(width, 256):
            rows = recv[:, :, start : start + size].reshape(SLOTS, size)
            mid[:, :, start : start + size] = (
                dot(to_home[p], rows).astype(BF16).reshape(RING, 32, size)
            )
        ring(
            ORDERS[p][1], lambda there: mid.at[there], lambda offset: mid_recv.at[offset - 1],
            send_sem, recv_sem,
        )

    def middle_sum(p, mid, mid_recv, sem):
        taken(mid_recv, sem)
        value = mid[place[ORDERS[p][1]]].astype(F32)
        for i in range(3):
            value = value + mid_recv[i].astype(F32)
        return value.reshape(RING, 8, value.shape[-1])

    def to_end(kind, p, top, low):
        send = end_send.at[kind, p]
        send[:, :, :LOW] = jnp.concatenate((top[:, :, :LOW], low), axis=1).astype(BF16)
        rest = top[:, :, LOW:]
        send[:, :, LOW:] = jnp.concatenate((rest, jnp.zeros_like(rest)), axis=1).astype(BF16)
        ring(
            ORDERS[p][0], lambda there: send.at[there],
            lambda offset: end_recv.at[kind, p, offset - 1],
            e1_send.at[kind], e1_recv.at[kind, p],
        )

    send_gradients(0)
    for p in PARTS:
        to_middle(
            p, out_recv.at[p], out_mid.at[p], out_mid_recv.at[p], CARRIED,
            m3_recv.at[p], m2_send.at[0], m2_recv.at[p],
        )
    send_gradients(1)
    for h in range(2):
        for p in PARTS:
            to_middle(
                p, in_recv[h].at[p], in_mid[h].at[p], in_mid_recv[h].at[p], (TOP, LOW)[h],
                g3_recv.at[h, p], g2_send.at[h], g2_recv.at[h, p],
            )
        if h == 0:
            for p in PARTS:
                value = middle_sum(p, out_mid.at[p], out_mid_recv.at[p], m2_recv.at[p])
                to_end(0, p, value[:, :, :TOP], value[:, :, TOP:])
    tops = [
        middle_sum(p, in_mid[0].at[p], in_mid_recv[0].at[p], g2_recv.at[0, p]) for p in PARTS
    ]
    for p in PARTS:
        low = middle_sum(p, in_mid[1].at[p], in_mid_recv[1].at[p], g2_recv.at[1, p])
        to_end(1, p, tops[p], low)

    for kind, out_ref in enumerate((mixed_ref, token_grads_ref)):
        for p in PARTS:
            taken(end_recv.at[kind, p], e1_recv.at[kind, p])
            value = end_send[kind, p, place[ORDERS[p][0]]].astype(F32)
            for i in range(3):
                value = value + end_recv[kind, p, i].astype(F32)
            cut = STARTS[p] + TOP
            out_ref[:, STARTS[p] : cut] = value[:8].astype(BF16)
            out_ref[:, cut : cut + LOWS[p]] = value[8:, : LOWS[p]].astype(BF16)
            if kind == 1 and p == 2:
                tile = value[8:, LOWS[p] : LOW]
                lane8 = iota((8, LANES), 1)
                column = iota((8, 8), 1)
                grads = jnp.zeros((8, 8), F32)
                for k in range(8):
                    hit = ids_ref[:, k : k + 1] == lane8 % EXPERTS
                    picked = jnp.sum(jnp.where(hit, tile, 0.0), axis=1, keepdims=True)
                    grads = jnp.where(column == k, picked, grads)
                gate_grads_ref[...] = grads

    for kind, rows in enumerate(kinds):
        taken(rows.at[:, 0, pl.ds(0, 3)], s1_send.at[kind])
        taken(rows.at[:, pl.ds(0, 3)], s2_send.at[kind])
        taken(end_send.at[kind, :, pl.ds(0, 3)], e1_send.at[kind])
    for h in range(2):
        taken(token_send[h].at[:, pl.ds(0, 7)], t3_send.at[h])
        taken(in_send[h].at[:, pl.ds(0, 7)], g3_send.at[h])
        taken(in_mid[h].at[:, pl.ds(0, 3)], g2_send.at[h])
    taken(grad_send.at[:, pl.ds(0, 7)], c3_send.at[0])
    taken(out_send.at[:, pl.ds(0, 7)], m3_send.at[0])
    taken(out_mid.at[:, pl.ds(0, 3)], m2_send.at[0])


def hand_over(*refs):
    for source, target in zip(refs[:3], refs[3:]):
        target[...] = source[...]


def shards(tokens, cotangent, expert_ids, gates, gate_weight, up_weight, down_weight):
    def vmem(shape, dtype=BF16):
        return pltpu.VMEM(shape, dtype)

    def parts(shape, widths, dtype=BF16):
        return [vmem((*shape, width), dtype) for width in widths]

    dma = pltpu.SemaphoreType.DMA
    block = (3, 8, 32)
    halves = (TOP, LOW)
    whole = pl.BlockSpec(memory_space=pltpu.VMEM)
    hbm = pl.BlockSpec(memory_space=pl.ANY)
    out_shape = (
        jax.ShapeDtypeStruct((8, WIDTH), BF16),
        jax.ShapeDtypeStruct((8, 8), F32),
        jax.ShapeDtypeStruct((8, WIDTH), BF16),
    )
    results = pl.pallas_call(
        kernel,
        out_shape=out_shape,
        in_specs=[hbm] * 7,
        out_specs=[whole] * 3,
        scratch_shapes=[
            vmem((8, WIDTH)),
            vmem((8, WIDTH)),
            vmem((8, 8), jnp.int32),
            vmem((8, 8), F32),
            vmem((WIDTH, HIDDEN)),
            vmem((WIDTH, HIDDEN)),
            vmem((HIDDEN, WIDTH)),
            vmem((3, RING, RING, 16, TOP)),
            vmem((3, RING, RING, 16, TOP)),
            parts(block, halves),
            parts(block, halves),
            vmem((*block, CARRIED)),
            vmem((*block, CARRIED)),
            vmem((4, SLOTS, HIDDEN), F32),
            vmem((*block, CARRIED)),
            vmem((*block, CARRIED)),
            parts(block, halves),
            parts(block, halves),
            vmem((3, RING, 32, CARRIED)),
            vmem((3, RING - 1, 32, CARRIED)),
            parts((3, RING, 32), halves),
            parts((3, RING - 1, 32), halves),
            vmem((2, 3, RING, 16, TOP)),
            vmem((2, 3, RING - 1, 16, TOP)),
            dma((4,)),
            dma((3,)),
            dma((2,)), dma((2, 3)), dma((2,)), dma((2, 3)),
            dma((2,)), dma((2, 3)), dma((1,)), dma((3,)),
            dma((1,)), dma((3,)), dma((2,)), dma((2, 3)),
            dma((1,)), dma((3,)), dma((2,)), dma((2, 3)),
            dma((2,)), dma((2, 3)),
        ],
        compiler_params=pltpu.CompilerParams(
            collective_id=0, has_side_effects=True, vmem_limit_bytes=60 * 2**20
        ),
    )(tokens, cotangent, expert_ids, gates, gate_weight, up_weight, down_weight)
    return pl.pallas_call(
        hand_over,
        out_shape=out_shape,
        in_specs=[whole] * 3,
        out_specs=[whole] * 3,
    )(*results)


def solution(mesh):
    rows = P(("ctx", "dp"), None)
    weights = P(("ctx", "dp"), None, None)
    return jax.shard_map(
        shards,
        mesh=mesh,
        in_specs=(rows, rows, rows, rows, weights, weights, weights),
        out_specs=(rows, rows, rows),
        check_vma=False,
    )
```

```python
import functools

import jax
import jax.numpy as jnp
from jax import lax
from jax.experimental import pallas as pl
from jax.experimental.pallas import tpu as pltpu
from jax.sharding import PartitionSpec as P

MESH = pl.DeviceIdType.MESH
BF16 = jnp.bfloat16
F32 = jnp.float32
LANES = 128
RING = 4
EXPERTS = 64
SLOTS = 256
HIDDEN = 768
WIDTH = 4096

ORDERS = ((2, 1, 0), (0, 2, 1), (1, 0, 2))
STARTS = (0, 1408, 2816)
WIDTHS = (1408, 1408, 1280)
TOP = 768
LOWS = (640, 640, 512)
LOW = 640
CARRIED = TOP + LOW
END = TOP // 2
PARTS = range(3)


def device_at(place, core):
    x, y, z = place
    return (x * 4 + (z % 2) * 2 + core, (z // 2) * 4 + y)


def expert_at(place, core):
    x, y, z = place
    return x * 16 + (z % 2) * 8 + core * 4 + (z // 2) * 2 + y // 2


def moved(place, axis, value):
    return tuple(value if i == axis else place[i] for i in range(3))


def iota(shape, axis):
    return lax.broadcasted_iota(jnp.int32, shape, axis)


def dot(a, b):
    return jnp.dot(a, b, preferred_element_type=F32)


def dot_nt(a, b):
    return lax.dot_general(a, b, (((1,), (1,)), ((), ())), preferred_element_type=F32)


def blocks(width, size):
    return [(i, min(size, width - i)) for i in range(0, width, size)]


def slot_coordinates(index, part):
    first, middle, last = ORDERS[part]
    coords = [None] * 3
    coords[last] = index // 64
    coords[middle] = (index // 8) % 4
    coords[first] = (index // 2) % 4
    return coords, (index // 32) % 2, index % 2


def index_in(part, coords, core, slot):
    first, middle, last = ORDERS[part]
    return coords[last] * 64 + core * 32 + coords[middle] * 8 + coords[first] * 2 + slot


def reorder(part, back):
    rows, cols = iota((SLOTS, SLOTS), 0), iota((SLOTS, SLOTS), 1)
    mine, other = (cols, rows) if back else (rows, cols)
    coords, core, slot = slot_coordinates(mine, part)
    return (index_in(0, coords, core, slot) == other).astype(F32).astype(BF16)


def kernel(
    tokens_hbm, cotangent_hbm, ids_hbm, gates_hbm, gate_hbm, up_hbm, down_hbm,
    mixed_ref, gate_grads_ref, token_grads_ref,
    tokens_ref, cotangent_ref, ids_ref, gates_ref, gate_w, up_w, down_w,
    token_rows, grad_rows, token_send, token_recv, grad_send, grad_recv,
    act, out_send, out_recv, in_send, in_recv,
    out_mid, out_mid_recv, in_mid, in_mid_recv, end_send, end_recv,
    input_sem, weight_sem,
    s1_send, s1_recv, s2_send, s2_recv, t3_send, t3_recv, c3_send, c3_recv,
    m3_send, m3_recv, g3_send, g3_recv, m2_send, m2_recv, g2_send, g2_recv, e1_send, e1_recv,
):
    ctx, dp = lax.axis_index("ctx"), lax.axis_index("dp")
    place = (ctx // 4, dp % 4, (dp // 4) * 2 + (ctx // 2) % 2)
    core = ctx % 2
    expert = expert_at(place, core)

    barrier = pltpu.get_barrier_semaphore()
    peers = [(place, 1 - core)]
    for axis in range(3):
        for offset in range(1, RING):
            there = moved(place, axis, (place[axis] + offset) % RING)
            peers += [(there, core), (there, 1 - core)]
    for there, its_core in peers:
        pl.semaphore_signal(
            barrier, inc=1, device_id=device_at(there, its_core), device_id_type=MESH
        )

    inputs = [
        pltpu.make_async_copy(src, dst, input_sem.at[i])
        for i, (src, dst) in enumerate(
            (
                (ids_hbm, ids_ref),
                (gates_hbm, gates_ref),
                (tokens_hbm, tokens_ref),
                (cotangent_hbm, cotangent_ref),
            )
        )
    ]
    for load in inputs:
        load.start()
    loads = [
        pltpu.make_async_copy(src.at[0], dst, weight_sem.at[i])
        for i, (src, dst) in enumerate(((gate_hbm, gate_w), (up_hbm, up_w), (down_hbm, down_w)))
    ]

    inputs[0].wait()
    inputs[1].wait()
    lane = iota((8, LANES), 1)
    named = jnp.zeros((8, LANES), F32)
    gate = jnp.zeros((8, LANES), F32)
    for k in range(8):
        hit = ids_ref[:, k : k + 1] == lane % EXPERTS
        named = jnp.where(hit, 1.0, named)
        gate = jnp.where(hit, gates_ref[:, k : k + 1], gate)
    row = iota((8, LANES), 0)
    before = jnp.zeros((8, LANES), F32)
    for i in range(7):
        before = before + jnp.where(row > i, named[i : i + 1, :], 0.0)
    slots = jnp.where(before == (lane // EXPERTS).astype(F32), named, 0.0)
    gate_high = gate.astype(BF16).astype(F32)
    gate_tile = jnp.where(lane < EXPERTS, gate_high, gate - gate_high)

    def stacked(ref, p, tiles):
        cut = STARTS[p] + TOP
        top = ref[:, STARTS[p] : cut].astype(F32)
        low = ref[:, cut : cut + LOWS[p]].astype(F32)
        return jnp.concatenate((top, jnp.concatenate((low, *tiles), axis=1)), axis=0).astype(BF16)

    inputs[2].wait()
    for p in PARTS:
        first, middle, last = ORDERS[p]
        tiles = (gate_tile, slots) if p == 2 else (slots,)
        token_rows[p, place[middle], place[first]] = stacked(tokens_ref, p, tiles)
    inputs[3].wait()
    for p in PARTS:
        first, middle, last = ORDERS[p]
        blank = jnp.zeros((8, TOP - LOWS[p]), F32)
        grad_rows[p, place[middle], place[first]] = stacked(cotangent_ref, p, (blank,))

    pl.semaphore_wait(barrier, len(peers))

    def taken(ref, sem):
        pltpu.make_async_copy(ref, ref, sem).wait()

    def ring(axis, source, target, send_sem, recv_sem):
        for offset in range(1, RING):
            there = moved(place, axis, (place[axis] + offset) % RING)
            pltpu.make_async_remote_copy(
                src_ref=source(there[axis]),
                dst_ref=target(offset),
                send_sem=send_sem,
                recv_sem=recv_sem,
                device_id=device_at(there, core),
                device_id_type=MESH,
            ).start()

    def exchange(axis, source, target, send_sem, recv_sem):
        mine = target.at[2 * place[axis] + core]
        for offset in (2, 1, 3, 0):
            there = moved(place, axis, (place[axis] + offset) % RING)
            for flip in range(2):
                its_core = core if flip == 0 else 1 - core
                block = source.at[2 * there[axis] + its_core]
                if offset == 0 and flip == 0:
                    pltpu.make_async_copy(block, mine, recv_sem).start()
                    continue
                pltpu.make_async_remote_copy(
                    src_ref=block,
                    dst_ref=mine,
                    send_sem=send_sem,
                    recv_sem=recv_sem,
                    device_id=device_at(there, its_core),
                    device_id_type=MESH,
                ).start()

    kinds = (token_rows, grad_rows)
    for kind, rows in enumerate(kinds):
        for p in PARTS:
            first, middle, last = ORDERS[p]
            home = rows.at[p, place[middle], place[first]]
            ring(
                first, lambda there: home, lambda offset: home,
                s1_send.at[kind], s1_recv.at[kind, p],
            )
    for load in loads:
        load.start()
    for kind, rows in enumerate(kinds):
        for p in PARTS:
            first, middle, last = ORDERS[p]
            home = rows.at[p, place[middle]]
            taken(rows.at[p, 0, pl.ds(0, 3)], s1_recv.at[kind, p])
            ring(
                middle, lambda there: home, lambda offset: home,
                s2_send.at[kind], s2_recv.at[kind, p],
            )

    r0, r1 = iota((SLOTS, SLOTS), 0), iota((SLOTS, SLOTS), 1)
    same = (r0 // 2) % 16 == r1 // 16
    half_masks = [same & ((r1 // 8) % 2 == h) for h in range(2)]
    u0, u1 = iota((SLOTS // 2, SLOTS), 0), iota((SLOTS // 2, SLOTS), 1)
    same_back = u0 // 8 == (u1 // 2) % 16
    lane = iota((SLOTS, LANES), 1)
    to_home, picks = [], []

    def pick_rows(p, h, rows, out, base, width):
        for start, size in blocks(width, 256):
            part = rows[p, :, :, :, start : start + size].reshape(SLOTS, size)
            out[:, :, base + start : base + start + size] = (
                dot(picks[p][h], part).astype(BF16).reshape(8, 32, size)
            )

    for p in PARTS:
        first, middle, last = ORDERS[p]
        taken(token_rows.at[p, pl.ds(0, 3)], s2_recv.at[0, p])
        index = iota((SLOTS, LANES), 0)
        wanted = expert_at(moved(place, last, index // 64), (index // 32) % 2)
        pick = (lane == (index % 2) * EXPERTS + wanted).astype(F32).astype(BF16)
        tile = token_rows[p, :, :, :, LOW:TOP].reshape(SLOTS, LANES)
        tile = tile.astype(F32).reshape(16, 2, 8, LANES)[:, 1]
        twice = jnp.concatenate((tile, tile), axis=1).reshape(SLOTS, LANES).astype(BF16)
        chosen = dot_nt(pick, twice)
        picks.append([jnp.where(mask, chosen, 0.0).astype(BF16) for mask in half_masks])
        home = dot_nt(tile.reshape(SLOTS // 2, LANES).astype(BF16), pick)
        to_home.append(jnp.where(same_back, home, 0.0).astype(BF16))
        pick_rows(p, 0, token_rows, token_send[0].at[p], 0, TOP)
        exchange(
            last, token_send[0].at[p], token_recv[0].at[p], t3_send.at[0], t3_recv.at[0, p]
        )
    for p in PARTS:
        pick_rows(p, 1, token_rows, token_send[1].at[p], 0, LOW)
        exchange(
            ORDERS[p][2], token_send[1].at[p], token_recv[1].at[p],
            t3_send.at[1], t3_recv.at[1, p],
        )
    for p in PARTS:
        taken(grad_rows.at[p, pl.ds(0, 3)], s2_recv.at[1, p])
        pick_rows(p, 0, grad_rows, grad_send.at[p], 0, TOP)
        pick_rows(p, 1, grad_rows, grad_send.at[p], TOP, LOW)
        exchange(
            ORDERS[p][2], grad_send.at[p], grad_recv.at[p], c3_send.at[0], c3_recv.at[p]
        )

    def in_order(p, rows):
        return rows if p == 0 else dot(reorder(p, True), rows).astype(BF16)

    gate_slot = None
    loads[0].wait()
    loads[1].wait()
    for h in range(2):
        for p in PARTS:
            taken(token_recv[h].at[p], t3_recv.at[h, p])
            rows = in_order(p, token_recv[h][p].reshape(SLOTS, (TOP, LOW)[h]))
            size = (TOP, LOWS[p])[h]
            if h == 1 and p == 2:
                tile = rows[:, size:].astype(F32)
                gate_slot = jnp.sum(
                    jnp.where(lane % EXPERTS == expert, tile, 0.0), axis=1, keepdims=True
                )
                rows = rows[:, :size]
            begin = STARTS[p] + h * TOP
            for i, weight in enumerate((gate_w, up_w)):
                for start, width in blocks(HIDDEN, 256):
                    value = dot(rows, weight[begin : begin + size, start : start + width])
                    if h == 0 and p == 0:
                        act[i, :, start : start + width] = value
                    else:
                        act[i, :, start : start + width] += value
    gate_act, second = act[0], act[1]
    squash = jax.nn.sigmoid(gate_act)
    hidden = gate_act * squash * second
    hidden_gated = (gate_slot * hidden).astype(BF16)
    act[2] = hidden
    loads[2].wait()

    def sent_order(p, value):
        return value if p == 0 else dot(reorder(p, False), value).astype(BF16)

    hidden_sent = [sent_order(p, hidden_gated) for p in PARTS]
    for h in range(2):
        for p in PARTS:
            width = (TOP, LOWS[p])[h]
            for start, size in blocks(width, 256):
                at = STARTS[p] + h * TOP + start
                out_send[h][p, :, :, start : start + size] = (
                    dot(hidden_sent[p], down_w[:, at : at + size])
                    .astype(BF16)
                    .reshape(8, 32, size)
                )
            if h == 1 and p == 2:
                out_send[h][p, :, :, width:] = jnp.zeros((8, 32, LANES), BF16)
            exchange(
                ORDERS[p][2], out_send[h].at[p], out_recv[h].at[p],
                m3_send.at[h], m3_recv.at[h, p],
            )

    for p in PARTS:
        taken(grad_recv.at[p], c3_recv.at[p])
        rows = in_order(p, grad_recv[p, :, :, : WIDTHS[p]].reshape(SLOTS, WIDTHS[p]))
        feats = slice(STARTS[p], STARTS[p] + WIDTHS[p])
        for start, size in blocks(HIDDEN, 256):
            value = dot_nt(rows, down_w[start : start + size, feats])
            if p == 0:
                act[3, :, start : start + size] = value
            else:
                act[3, :, start : start + size] += value
    backward = act[3]
    gate_act, second = act[0], act[1]
    squash = jax.nn.sigmoid(gate_act)
    gate_grad = jnp.sum(backward * act[2], axis=1, keepdims=True)
    scaled = backward * gate_slot * squash
    grad_gate = (scaled * second * (1.0 + gate_act * (1.0 - squash))).astype(BF16)
    grad_second = (scaled * gate_act).astype(BF16)
    grad_high = gate_grad.astype(BF16).astype(F32)
    grad_tile = jnp.where(
        lane == expert, grad_high, jnp.where(lane == expert + EXPERTS, gate_grad - grad_high, 0.0)
    ).astype(BF16)
    sent_gate = [sent_order(p, grad_gate) for p in PARTS]
    sent_second = [sent_order(p, grad_second) for p in PARTS]

    def send_gradients(h):
        for p in PARTS:
            width = (TOP, LOWS[p])[h]
            for start, size in blocks(width, 256):
                at = STARTS[p] + h * TOP + start
                value = dot_nt(sent_gate[p], gate_w[at : at + size, :]) + dot_nt(
                    sent_second[p], up_w[at : at + size, :]
                )
                in_send[h][p, :, :, start : start + size] = value.astype(BF16).reshape(8, 32, size)
            if h == 1 and p == 2:
                in_send[h][p, :, :, width:] = sent_order(p, grad_tile).reshape(8, 32, LANES)
            exchange(
                ORDERS[p][2], in_send[h].at[p], in_recv[h].at[p],
                g3_send.at[h], g3_recv.at[h, p],
            )

    def slot_sum(p, recv, mid, width, sem):
        taken(recv, sem)
        for start, size in blocks(width, 256):
            rows = recv[:, :, start : start + size].reshape(SLOTS, size)
            mid[:, :, start : start + size] = (
                dot(to_home[p], rows).astype(BF16).reshape(RING, 32, size)
            )

    def to_middle(p, mid, mid_recv, send_sem, recv_sem):
        ring(
            ORDERS[p][1], lambda there: mid.at[there], lambda offset: mid_recv.at[offset - 1],
            send_sem, recv_sem,
        )

    def middle_sum(p, mid, mid_recv, sem):
        taken(mid_recv, sem)
        value = mid[place[ORDERS[p][1]]].astype(F32)
        for i in range(3):
            value = value + mid_recv[i].astype(F32)
        return value.reshape(RING, 8, value.shape[-1])

    def end_pack(kind, p, h, value):
        rest = value[:, :, END:]
        if h == 1:
            rest = jnp.concatenate((rest, jnp.zeros((RING, 8, TOP - LOW), F32)), axis=2)
        end_send[kind, p, :, :, h * END : (h + 1) * END] = jnp.concatenate(
            (value[:, :, :END], rest), axis=1
        ).astype(BF16)

    def to_end(kind, p, cols, send_sem, recv_sem):
        send = end_send.at[kind, p]
        ring(
            ORDERS[p][0], lambda there: send.at[there, :, cols],
            lambda offset: end_recv.at[kind, p, offset - 1, :, cols], send_sem, recv_sem,
        )

    end_cols = (pl.ds(0, END), pl.ds(END, END))
    send_gradients(0)
    send_gradients(1)
    for h in range(2):
        for p in PARTS:
            mid = in_mid[h].at[p]
            slot_sum(p, in_recv[h].at[p], mid, (TOP, LOW)[h], g3_recv.at[h, p])
            to_middle(p, mid, in_mid_recv[h].at[p], g2_send.at[h], g2_recv.at[h, p])
        if h == 0:
            for p in PARTS:
                for i in range(2):
                    width = (TOP, LOW)[i]
                    mid = out_mid.at[p, :, :, pl.ds(i * TOP, width)]
                    slot_sum(p, out_recv[i].at[p], mid, width, m3_recv.at[i, p])
                to_middle(p, out_mid.at[p], out_mid_recv.at[p], m2_send.at[0], m2_recv.at[p])

    def end_gradients(h):
        for p in PARTS:
            value = middle_sum(p, in_mid[h].at[p], in_mid_recv[h].at[p], g2_recv.at[h, p])
            end_pack(1, p, h, value)
            to_end(1, p, end_cols[h], e1_send.at[h], e1_recv.at[h, p])

    end_gradients(0)
    for p in PARTS:
        value = middle_sum(p, out_mid.at[p], out_mid_recv.at[p], m2_recv.at[p])
        end_pack(0, p, 0, value[:, :, :TOP])
        end_pack(0, p, 1, value[:, :, TOP:])
        to_end(0, p, pl.ds(0, TOP), e1_send.at[2], e1_recv.at[2, p])
    end_gradients(1)

    def finish(kind, out_ref, p, h):
        cols = end_cols[h]
        value = end_send[kind, p, place[ORDERS[p][0]], :, cols].astype(F32)
        for i in range(3):
            value = value + end_recv[kind, p, i, :, cols].astype(F32)
        begin = STARTS[p] + h * TOP
        rest = (TOP, LOWS[p])[h] - END
        out_ref[:, begin : begin + END] = value[:8].astype(BF16)
        out_ref[:, begin + END : begin + END + rest] = value[8:, :rest].astype(BF16)
        return value[8:, rest : rest + LANES]

    for p in PARTS:
        taken(end_recv.at[0, p], e1_recv.at[2, p])
        for h in range(2):
            finish(0, mixed_ref, p, h)
    for h in range(2):
        for p in PARTS:
            taken(end_recv.at[1, p, :, :, end_cols[h]], e1_recv.at[h, p])
            tile = finish(1, token_grads_ref, p, h)
    lane8 = iota((8, LANES), 1)
    column = iota((8, 8), 1)
    grads = jnp.zeros((8, 8), F32)
    for k in range(8):
        hit = ids_ref[:, k : k + 1] == lane8 % EXPERTS
        picked = jnp.sum(jnp.where(hit, tile, 0.0), axis=1, keepdims=True)
        grads = jnp.where(column == k, picked, grads)
    gate_grads_ref[...] = grads

    for kind, rows in enumerate(kinds):
        taken(rows.at[:, 0, pl.ds(0, 3)], s1_send.at[kind])
        taken(rows.at[:, pl.ds(0, 3)], s2_send.at[kind])
    for h in range(2):
        taken(token_send[h].at[:, pl.ds(0, 7)], t3_send.at[h])
        taken(in_send[h].at[:, pl.ds(0, 7)], g3_send.at[h])
        taken(in_mid[h].at[:, pl.ds(0, 3)], g2_send.at[h])
        taken(out_send[h].at[:, pl.ds(0, 7)], m3_send.at[h])
        taken(end_send.at[1, :, pl.ds(0, 3), :, end_cols[h]], e1_send.at[h])
    taken(grad_send.at[:, pl.ds(0, 7)], c3_send.at[0])
    taken(end_send.at[0, :, pl.ds(0, 3)], e1_send.at[2])
    taken(out_mid.at[:, pl.ds(0, 3)], m2_send.at[0])


def hand_over(*refs):
    for source, target in zip(refs[:3], refs[3:]):
        target[...] = source[...]


def shards(tokens, cotangent, expert_ids, gates, gate_weight, up_weight, down_weight):
    def vmem(shape, dtype=BF16):
        return pltpu.VMEM(shape, dtype)

    def parts(shape, widths, dtype=BF16):
        return [vmem((*shape, width), dtype) for width in widths]

    dma = pltpu.SemaphoreType.DMA
    block = (3, 8, 32)
    halves = (TOP, LOW)
    whole = pl.BlockSpec(memory_space=pltpu.VMEM)
    hbm = pl.BlockSpec(memory_space=pl.ANY)
    out_shape = (
        jax.ShapeDtypeStruct((8, WIDTH), BF16),
        jax.ShapeDtypeStruct((8, 8), F32),
        jax.ShapeDtypeStruct((8, WIDTH), BF16),
    )
    results = pl.pallas_call(
        kernel,
        out_shape=out_shape,
        in_specs=[hbm] * 7,
        out_specs=[whole] * 3,
        scratch_shapes=[
            vmem((8, WIDTH)),
            vmem((8, WIDTH)),
            vmem((8, 8), jnp.int32),
            vmem((8, 8), F32),
            vmem((WIDTH, HIDDEN)),
            vmem((WIDTH, HIDDEN)),
            vmem((HIDDEN, WIDTH)),
            vmem((3, RING, RING, 16, TOP)),
            vmem((3, RING, RING, 16, TOP)),
            parts(block, halves),
            parts(block, halves),
            vmem((*block, CARRIED)),
            vmem((*block, CARRIED)),
            vmem((4, SLOTS, HIDDEN), F32),
            parts(block, halves),
            parts(block, halves),
            parts(block, halves),
            parts(block, halves),
            vmem((3, RING, 32, CARRIED)),
            vmem((3, RING - 1, 32, CARRIED)),
            parts((3, RING, 32), halves),
            parts((3, RING - 1, 32), halves),
            vmem((2, 3, RING, 16, TOP)),
            vmem((2, 3, RING - 1, 16, TOP)),
            dma((4,)),
            dma((3,)),
            dma((2,)), dma((2, 3)), dma((2,)), dma((2, 3)),
            dma((2,)), dma((2, 3)), dma((1,)), dma((3,)),
            dma((2,)), dma((2, 3)), dma((2,)), dma((2, 3)),
            dma((1,)), dma((3,)), dma((2,)), dma((2, 3)),
            dma((3,)), dma((3, 3)),
        ],
        compiler_params=pltpu.CompilerParams(
            collective_id=0, has_side_effects=True, vmem_limit_bytes=60 * 2**20
        ),
    )(tokens, cotangent, expert_ids, gates, gate_weight, up_weight, down_weight)
    return pl.pallas_call(
        hand_over,
        out_shape=out_shape,
        in_specs=[whole] * 3,
        out_specs=[whole] * 3,
    )(*results)


def solution(mesh):
    rows = P(("ctx", "dp"), None)
    weights = P(("ctx", "dp"), None, None)
    return jax.shard_map(
        shards,
        mesh=mesh,
        in_specs=(rows, rows, rows, rows, weights, weights, weights),
        out_specs=(rows, rows, rows),
        check_vma=False,
    )
```

```python
import functools

import jax
import jax.numpy as jnp
from jax import lax
from jax.experimental import pallas as pl
from jax.experimental.pallas import tpu as pltpu
from jax.sharding import PartitionSpec as P

MESH = pl.DeviceIdType.MESH
BF16 = jnp.bfloat16
F32 = jnp.float32
LANES = 128
RING = 4
EXPERTS = 64
SLOTS = 256
HIDDEN = 768
WIDTH = 4096

ORDERS = ((2, 1, 0), (0, 2, 1), (1, 0, 2))
STARTS = (0, 1408, 2816)
WIDTHS = (1408, 1408, 1280)
TOP = 768
LOWS = (640, 640, 512)
LOW = 640
CARRIED = TOP + LOW
CUTS = ((512, 896), (768, 640), (896, 512))
ENDS = ((256, 512), (384, 384))
PARTS = range(3)


def device_at(place, core):
    x, y, z = place
    return (x * 4 + (z % 2) * 2 + core, (z // 2) * 4 + y)


def expert_at(place, core):
    x, y, z = place
    return x * 16 + (z % 2) * 8 + core * 4 + (z // 2) * 2 + y // 2


def moved(place, axis, value):
    return tuple(value if i == axis else place[i] for i in range(3))


def piece_width(kind, part, piece):
    return CUTS[kind][0] if piece == 0 else WIDTHS[part] - CUTS[kind][0]


def iota(shape, axis):
    return lax.broadcasted_iota(jnp.int32, shape, axis)


def dot(a, b):
    return jnp.dot(a, b, preferred_element_type=F32)


def dot_nt(a, b):
    return lax.dot_general(a, b, (((1,), (1,)), ((), ())), preferred_element_type=F32)


def blocks(width, size):
    return [(i, min(size, width - i)) for i in range(0, width, size)]


def slot_coordinates(index, part):
    first, middle, last = ORDERS[part]
    coords = [None] * 3
    coords[last] = index // 64
    coords[middle] = (index // 8) % 4
    coords[first] = (index // 2) % 4
    return coords, (index // 32) % 2, index % 2


def index_in(part, coords, core, slot):
    first, middle, last = ORDERS[part]
    return coords[last] * 64 + core * 32 + coords[middle] * 8 + coords[first] * 2 + slot


def reorder(part, back):
    rows, cols = iota((SLOTS, SLOTS), 0), iota((SLOTS, SLOTS), 1)
    mine, other = (cols, rows) if back else (rows, cols)
    coords, core, slot = slot_coordinates(mine, part)
    return (index_in(0, coords, core, slot) == other).astype(F32).astype(BF16)


def kernel(
    tokens_hbm, cotangent_hbm, ids_hbm, gates_hbm, gate_hbm, up_hbm, down_hbm,
    mixed_ref, gate_grads_ref, token_grads_ref,
    tokens_ref, cotangent_ref, ids_ref, gates_ref, gate_w, up_w, down_w,
    token_rows, grad_rows, token_send, token_recv, grad_send, grad_recv,
    act, out_send, out_recv, in_send, in_recv,
    out_mid, out_mid_recv, in_mid, in_mid_recv, end_send, end_recv,
    input_sem, weight_sem,
    s1_send, s1_recv, s2_send, s2_recv, t3_send, t3_recv, c3_send, c3_recv,
    m3_send, m3_recv, g3_send, g3_recv, m2_send, m2_recv, g2_send, g2_recv, e1_send, e1_recv,
):
    ctx, dp = lax.axis_index("ctx"), lax.axis_index("dp")
    place = (ctx // 4, dp % 4, (dp // 4) * 2 + (ctx // 2) % 2)
    core = ctx % 2
    expert = expert_at(place, core)

    barrier = pltpu.get_barrier_semaphore()
    peers = [(place, 1 - core)]
    for axis in range(3):
        for offset in range(1, RING):
            there = moved(place, axis, (place[axis] + offset) % RING)
            peers += [(there, core), (there, 1 - core)]
    for there, its_core in peers:
        pl.semaphore_signal(
            barrier, inc=1, device_id=device_at(there, its_core), device_id_type=MESH
        )

    inputs = [
        pltpu.make_async_copy(src, dst, input_sem.at[i])
        for i, (src, dst) in enumerate(
            (
                (ids_hbm, ids_ref),
                (gates_hbm, gates_ref),
                (tokens_hbm, tokens_ref),
                (cotangent_hbm, cotangent_ref),
            )
        )
    ]
    for load in inputs:
        load.start()
    loads = [
        pltpu.make_async_copy(src.at[0], dst, weight_sem.at[i])
        for i, (src, dst) in enumerate(((gate_hbm, gate_w), (up_hbm, up_w), (down_hbm, down_w)))
    ]

    inputs[0].wait()
    inputs[1].wait()
    lane = iota((8, LANES), 1)
    named = jnp.zeros((8, LANES), F32)
    gate = jnp.zeros((8, LANES), F32)
    for k in range(8):
        hit = ids_ref[:, k : k + 1] == lane % EXPERTS
        named = jnp.where(hit, 1.0, named)
        gate = jnp.where(hit, gates_ref[:, k : k + 1], gate)
    row = iota((8, LANES), 0)
    before = jnp.zeros((8, LANES), F32)
    for i in range(7):
        before = before + jnp.where(row > i, named[i : i + 1, :], 0.0)
    slots = jnp.where(before == (lane // EXPERTS).astype(F32), named, 0.0)
    gate_high = gate.astype(BF16).astype(F32)
    gate_tile = jnp.where(lane < EXPERTS, gate_high, gate - gate_high)

    def stacked(ref, p, tiles):
        cut = STARTS[p] + TOP
        top = ref[:, STARTS[p] : cut].astype(F32)
        low = ref[:, cut : cut + LOWS[p]].astype(F32)
        return jnp.concatenate((top, jnp.concatenate((low, *tiles), axis=1)), axis=0).astype(BF16)

    inputs[2].wait()
    for p in PARTS:
        first, middle, last = ORDERS[p]
        tiles = (gate_tile, slots) if p == 2 else (slots,)
        token_rows[p, place[middle], place[first]] = stacked(tokens_ref, p, tiles)
    inputs[3].wait()
    for p in PARTS:
        first, middle, last = ORDERS[p]
        blank = jnp.zeros((8, TOP - LOWS[p]), F32)
        grad_rows[p, place[middle], place[first]] = stacked(cotangent_ref, p, (blank,))

    pl.semaphore_wait(barrier, len(peers))

    def taken(ref, sem):
        pltpu.make_async_copy(ref, ref, sem).wait()

    def ring(axis, source, target, send_sem, recv_sem):
        for offset in range(1, RING):
            there = moved(place, axis, (place[axis] + offset) % RING)
            pltpu.make_async_remote_copy(
                src_ref=source(there[axis]),
                dst_ref=target(offset),
                send_sem=send_sem,
                recv_sem=recv_sem,
                device_id=device_at(there, core),
                device_id_type=MESH,
            ).start()

    def exchange(axis, source, target, send_sem, recv_sem):
        mine = target.at[2 * place[axis] + core]
        for offset in (2, 1, 3, 0):
            there = moved(place, axis, (place[axis] + offset) % RING)
            for flip in range(2):
                its_core = core if flip == 0 else 1 - core
                block = source.at[2 * there[axis] + its_core]
                if offset == 0 and flip == 0:
                    pltpu.make_async_copy(block, mine, recv_sem).start()
                    continue
                pltpu.make_async_remote_copy(
                    src_ref=block,
                    dst_ref=mine,
                    send_sem=send_sem,
                    recv_sem=recv_sem,
                    device_id=device_at(there, its_core),
                    device_id_type=MESH,
                ).start()

    kinds = (token_rows, grad_rows)
    for kind, rows in enumerate(kinds):
        for p in PARTS:
            first, middle, last = ORDERS[p]
            home = rows.at[p, place[middle], place[first]]
            ring(
                first, lambda there: home, lambda offset: home,
                s1_send.at[kind], s1_recv.at[kind, p],
            )
    for load in loads:
        load.start()
    for kind, rows in enumerate(kinds):
        for p in PARTS:
            first, middle, last = ORDERS[p]
            home = rows.at[p, place[middle]]
            taken(rows.at[p, 0, pl.ds(0, 3)], s1_recv.at[kind, p])
            ring(
                middle, lambda there: home, lambda offset: home,
                s2_send.at[kind], s2_recv.at[kind, p],
            )

    r0, r1 = iota((SLOTS, SLOTS), 0), iota((SLOTS, SLOTS), 1)
    same = (r0 // 2) % 16 == r1 // 16
    half_masks = [same & ((r1 // 8) % 2 == h) for h in range(2)]
    u0, u1 = iota((SLOTS // 2, SLOTS), 0), iota((SLOTS // 2, SLOTS), 1)
    same_back = u0 // 8 == (u1 // 2) % 16
    lane = iota((SLOTS, LANES), 1)
    to_home, picks = [], []

    def pick_rows(p, h, rows, out, base, width, skip=0):
        for start, size in blocks(width, 256):
            cols = slice(skip + start, skip + start + size)
            part = rows[p, :, :, :, cols].reshape(SLOTS, size)
            out[:, :, base + start : base + start + size] = (
                dot(picks[p][h], part).astype(BF16).reshape(8, 32, size)
            )

    def pick_piece(p, piece):
        begin = piece * CUTS[2][0]
        end = begin + CUTS[2][piece]
        for half, (low, high) in enumerate(((0, TOP), (TOP, CARRIED))):
            left, right = max(begin, low), min(end, high)
            if left < right:
                pick_rows(
                    p, half, token_rows, token_send[piece].at[p], left - begin, right - left,
                    left - low,
                )

    for p in PARTS:
        first, middle, last = ORDERS[p]
        taken(token_rows.at[p, pl.ds(0, 3)], s2_recv.at[0, p])
        index = iota((SLOTS, LANES), 0)
        wanted = expert_at(moved(place, last, index // 64), (index // 32) % 2)
        pick = (lane == (index % 2) * EXPERTS + wanted).astype(F32).astype(BF16)
        tile = token_rows[p, :, :, :, LOW:TOP].reshape(SLOTS, LANES)
        tile = tile.astype(F32).reshape(16, 2, 8, LANES)[:, 1]
        twice = jnp.concatenate((tile, tile), axis=1).reshape(SLOTS, LANES).astype(BF16)
        chosen = dot_nt(pick, twice)
        picks.append([jnp.where(mask, chosen, 0.0).astype(BF16) for mask in half_masks])
        home = dot_nt(tile.reshape(SLOTS // 2, LANES).astype(BF16), pick)
        to_home.append(jnp.where(same_back, home, 0.0).astype(BF16))
        pick_piece(p, 0)
        exchange(
            last, token_send[0].at[p], token_recv[0].at[p], t3_send.at[0], t3_recv.at[0, p]
        )
    for p in PARTS:
        pick_piece(p, 1)
        exchange(
            ORDERS[p][2], token_send[1].at[p], token_recv[1].at[p],
            t3_send.at[1], t3_recv.at[1, p],
        )
    for p in PARTS:
        taken(grad_rows.at[p, pl.ds(0, 3)], s2_recv.at[1, p])
        pick_rows(p, 0, grad_rows, grad_send.at[p], 0, TOP)
        pick_rows(p, 1, grad_rows, grad_send.at[p], TOP, LOW)
        exchange(
            ORDERS[p][2], grad_send.at[p], grad_recv.at[p], c3_send.at[0], c3_recv.at[p]
        )

    def in_order(p, rows):
        return rows if p == 0 else dot(reorder(p, True), rows).astype(BF16)

    gate_slot = None
    loads[0].wait()
    loads[1].wait()
    for h in range(2):
        for p in PARTS:
            taken(token_recv[h].at[p], t3_recv.at[h, p])
            rows = in_order(p, token_recv[h][p].reshape(SLOTS, CUTS[2][h]))
            size = piece_width(2, p, h)
            if h == 1 and p == 2:
                tile = rows[:, size:].astype(F32)
                gate_slot = jnp.sum(
                    jnp.where(lane % EXPERTS == expert, tile, 0.0), axis=1, keepdims=True
                )
                rows = rows[:, :size]
            begin = STARTS[p] + h * CUTS[2][0]
            for i, weight in enumerate((gate_w, up_w)):
                for start, width in blocks(HIDDEN, 256):
                    value = dot(rows, weight[begin : begin + size, start : start + width])
                    if h == 0 and p == 0:
                        act[i, :, start : start + width] = value
                    else:
                        act[i, :, start : start + width] += value
    gate_act, second = act[0], act[1]
    squash = jax.nn.sigmoid(gate_act)
    hidden = gate_act * squash * second
    hidden_gated = (gate_slot * hidden).astype(BF16)
    act[2] = hidden
    loads[2].wait()

    def sent_order(p, value):
        return value if p == 0 else dot(reorder(p, False), value).astype(BF16)

    hidden_sent = [sent_order(p, hidden_gated) for p in PARTS]
    for h in range(2):
        for p in PARTS:
            width = piece_width(0, p, h)
            for start, size in blocks(width, 256):
                at = STARTS[p] + h * CUTS[0][0] + start
                out_send[h][p, :, :, start : start + size] = (
                    dot(hidden_sent[p], down_w[:, at : at + size])
                    .astype(BF16)
                    .reshape(8, 32, size)
                )
            if h == 1 and p == 2:
                out_send[h][p, :, :, width:] = jnp.zeros((8, 32, LANES), BF16)
            exchange(
                ORDERS[p][2], out_send[h].at[p], out_recv[h].at[p],
                m3_send.at[h], m3_recv.at[h, p],
            )

    for p in PARTS:
        taken(grad_recv.at[p], c3_recv.at[p])
        rows = in_order(p, grad_recv[p, :, :, : WIDTHS[p]].reshape(SLOTS, WIDTHS[p]))
        feats = slice(STARTS[p], STARTS[p] + WIDTHS[p])
        for start, size in blocks(HIDDEN, 256):
            value = dot_nt(rows, down_w[start : start + size, feats])
            if p == 0:
                act[3, :, start : start + size] = value
            else:
                act[3, :, start : start + size] += value
    backward = act[3]
    gate_act, second = act[0], act[1]
    squash = jax.nn.sigmoid(gate_act)
    gate_grad = jnp.sum(backward * act[2], axis=1, keepdims=True)
    scaled = backward * gate_slot * squash
    grad_gate = (scaled * second * (1.0 + gate_act * (1.0 - squash))).astype(BF16)
    grad_second = (scaled * gate_act).astype(BF16)
    grad_high = gate_grad.astype(BF16).astype(F32)
    grad_tile = jnp.where(
        lane == expert, grad_high, jnp.where(lane == expert + EXPERTS, gate_grad - grad_high, 0.0)
    ).astype(BF16)
    sent_gate = [sent_order(p, grad_gate) for p in PARTS]
    sent_second = [sent_order(p, grad_second) for p in PARTS]

    def send_gradients(h):
        for p in PARTS:
            width = piece_width(1, p, h)
            for start, size in blocks(width, 256):
                at = STARTS[p] + h * CUTS[1][0] + start
                value = dot_nt(sent_gate[p], gate_w[at : at + size, :]) + dot_nt(
                    sent_second[p], up_w[at : at + size, :]
                )
                in_send[h][p, :, :, start : start + size] = value.astype(BF16).reshape(8, 32, size)
            if h == 1 and p == 2:
                in_send[h][p, :, :, width:] = sent_order(p, grad_tile).reshape(8, 32, LANES)
            exchange(
                ORDERS[p][2], in_send[h].at[p], in_recv[h].at[p],
                g3_send.at[h], g3_recv.at[h, p],
            )

    def slot_sum(p, recv, mid, width, sem):
        taken(recv, sem)
        for start, size in blocks(width, 256):
            rows = recv[:, :, start : start + size].reshape(SLOTS, size)
            mid[:, :, start : start + size] = (
                dot(to_home[p], rows).astype(BF16).reshape(RING, 32, size)
            )

    def to_middle(p, mid, mid_recv, send_sem, recv_sem):
        ring(
            ORDERS[p][1], lambda there: mid.at[there], lambda offset: mid_recv.at[offset - 1],
            send_sem, recv_sem,
        )

    def middle_sum(p, mid, mid_recv, sem):
        taken(mid_recv, sem)
        value = mid[place[ORDERS[p][1]]].astype(F32)
        for i in range(3):
            value = value + mid_recv[i].astype(F32)
        return value.reshape(RING, 8, value.shape[-1])

    def end_cols(kind, h):
        return slice(h * ENDS[kind][0], h * ENDS[kind][0] + ENDS[kind][h])

    def end_pack(kind, p, h, value):
        size = ENDS[kind][h]
        rest = value[:, :, size:]
        if rest.shape[2] < size:
            blank = jnp.zeros((RING, 8, size - rest.shape[2]), F32)
            rest = jnp.concatenate((rest, blank), axis=2)
        end_send[kind, p, :, :, end_cols(kind, h)] = jnp.concatenate(
            (value[:, :, :size], rest), axis=1
        ).astype(BF16)

    def to_end(kind, p, cols, send_sem, recv_sem):
        send = end_send.at[kind, p]
        ring(
            ORDERS[p][0], lambda there: send.at[there, :, cols],
            lambda offset: end_recv.at[kind, p, offset - 1, :, cols], send_sem, recv_sem,
        )

    send_gradients(0)
    send_gradients(1)
    for h in range(2):
        for p in PARTS:
            mid = in_mid[h].at[p]
            slot_sum(p, in_recv[h].at[p], mid, CUTS[1][h], g3_recv.at[h, p])
            to_middle(p, mid, in_mid_recv[h].at[p], g2_send.at[h], g2_recv.at[h, p])
        if h == 0:
            for p in PARTS:
                for i in range(2):
                    width = CUTS[0][i]
                    mid = out_mid.at[p, :, :, pl.ds(i * CUTS[0][0], width)]
                    slot_sum(p, out_recv[i].at[p], mid, width, m3_recv.at[i, p])
                to_middle(p, out_mid.at[p], out_mid_recv.at[p], m2_send.at[0], m2_recv.at[p])

    def end_gradients(h):
        for p in PARTS:
            value = middle_sum(p, in_mid[h].at[p], in_mid_recv[h].at[p], g2_recv.at[h, p])
            end_pack(1, p, h, value)
            to_end(1, p, end_cols(1, h), e1_send.at[h], e1_recv.at[h, p])

    end_gradients(0)
    for p in PARTS:
        value = middle_sum(p, out_mid.at[p], out_mid_recv.at[p], m2_recv.at[p])
        end_pack(0, p, 0, value[:, :, : CUTS[0][0]])
        end_pack(0, p, 1, value[:, :, CUTS[0][0] :])
        to_end(0, p, slice(0, TOP), e1_send.at[2], e1_recv.at[2, p])
    end_gradients(1)

    def finish(kind, out_ref, p, h):
        cols = end_cols(kind, h)
        value = end_send[kind, p, place[ORDERS[p][0]], :, cols].astype(F32)
        for i in range(3):
            value = value + end_recv[kind, p, i, :, cols].astype(F32)
        begin = STARTS[p] + h * CUTS[kind][0]
        size = ENDS[kind][h]
        rest = piece_width(kind, p, h) - size
        out_ref[:, begin : begin + size] = value[:8].astype(BF16)
        if rest > 0:
            out_ref[:, begin + size : begin + size + rest] = value[8:, :rest].astype(BF16)
        return value[8:, rest : rest + LANES]

    for p in PARTS:
        taken(end_recv.at[0, p], e1_recv.at[2, p])
        for h in range(2):
            finish(0, mixed_ref, p, h)
    for h in range(2):
        for p in PARTS:
            taken(end_recv.at[1, p, :, :, end_cols(1, h)], e1_recv.at[h, p])
            tile = finish(1, token_grads_ref, p, h)
    lane8 = iota((8, LANES), 1)
    column = iota((8, 8), 1)
    grads = jnp.zeros((8, 8), F32)
    for k in range(8):
        hit = ids_ref[:, k : k + 1] == lane8 % EXPERTS
        picked = jnp.sum(jnp.where(hit, tile, 0.0), axis=1, keepdims=True)
        grads = jnp.where(column == k, picked, grads)
    gate_grads_ref[...] = grads

    for kind, rows in enumerate(kinds):
        taken(rows.at[:, 0, pl.ds(0, 3)], s1_send.at[kind])
        taken(rows.at[:, pl.ds(0, 3)], s2_send.at[kind])
    for h in range(2):
        taken(token_send[h].at[:, pl.ds(0, 7)], t3_send.at[h])
        taken(in_send[h].at[:, pl.ds(0, 7)], g3_send.at[h])
        taken(in_mid[h].at[:, pl.ds(0, 3)], g2_send.at[h])
        taken(out_send[h].at[:, pl.ds(0, 7)], m3_send.at[h])
        taken(end_send.at[1, :, pl.ds(0, 3), :, end_cols(1, h)], e1_send.at[h])
    taken(grad_send.at[:, pl.ds(0, 7)], c3_send.at[0])
    taken(end_send.at[0, :, pl.ds(0, 3)], e1_send.at[2])
    taken(out_mid.at[:, pl.ds(0, 3)], m2_send.at[0])


def hand_over(*refs):
    for source, target in zip(refs[:3], refs[3:]):
        target[...] = source[...]


def shards(tokens, cotangent, expert_ids, gates, gate_weight, up_weight, down_weight):
    def vmem(shape, dtype=BF16):
        return pltpu.VMEM(shape, dtype)

    def parts(shape, widths, dtype=BF16):
        return [vmem((*shape, width), dtype) for width in widths]

    dma = pltpu.SemaphoreType.DMA
    block = (3, 8, 32)
    whole = pl.BlockSpec(memory_space=pltpu.VMEM)
    hbm = pl.BlockSpec(memory_space=pl.ANY)
    out_shape = (
        jax.ShapeDtypeStruct((8, WIDTH), BF16),
        jax.ShapeDtypeStruct((8, 8), F32),
        jax.ShapeDtypeStruct((8, WIDTH), BF16),
    )
    results = pl.pallas_call(
        kernel,
        out_shape=out_shape,
        in_specs=[hbm] * 7,
        out_specs=[whole] * 3,
        scratch_shapes=[
            vmem((8, WIDTH)),
            vmem((8, WIDTH)),
            vmem((8, 8), jnp.int32),
            vmem((8, 8), F32),
            vmem((WIDTH, HIDDEN)),
            vmem((WIDTH, HIDDEN)),
            vmem((HIDDEN, WIDTH)),
            vmem((3, RING, RING, 16, TOP)),
            vmem((3, RING, RING, 16, TOP)),
            parts(block, CUTS[2]),
            parts(block, CUTS[2]),
            vmem((*block, CARRIED)),
            vmem((*block, CARRIED)),
            vmem((4, SLOTS, HIDDEN), F32),
            parts(block, CUTS[0]),
            parts(block, CUTS[0]),
            parts(block, CUTS[1]),
            parts(block, CUTS[1]),
            vmem((3, RING, 32, CARRIED)),
            vmem((3, RING - 1, 32, CARRIED)),
            parts((3, RING, 32), CUTS[1]),
            parts((3, RING - 1, 32), CUTS[1]),
            vmem((2, 3, RING, 16, TOP)),
            vmem((2, 3, RING - 1, 16, TOP)),
            dma((4,)),
            dma((3,)),
            dma((2,)), dma((2, 3)), dma((2,)), dma((2, 3)),
            dma((2,)), dma((2, 3)), dma((1,)), dma((3,)),
            dma((2,)), dma((2, 3)), dma((2,)), dma((2, 3)),
            dma((1,)), dma((3,)), dma((2,)), dma((2, 3)),
            dma((3,)), dma((3, 3)),
        ],
        compiler_params=pltpu.CompilerParams(
            collective_id=0, has_side_effects=True, vmem_limit_bytes=60 * 2**20
        ),
    )(tokens, cotangent, expert_ids, gates, gate_weight, up_weight, down_weight)
    return pl.pallas_call(
        hand_over,
        out_shape=out_shape,
        in_specs=[whole] * 3,
        out_specs=[whole] * 3,
    )(*results)


def solution(mesh):
    rows = P(("ctx", "dp"), None)
    weights = P(("ctx", "dp"), None, None)
    return jax.shard_map(
        shards,
        mesh=mesh,
        in_specs=(rows, rows, rows, rows, weights, weights, weights),
        out_specs=(rows, rows, rows),
        check_vma=False,
    )
```

```python
import functools

import jax
import jax.numpy as jnp
from jax import lax
from jax.experimental import pallas as pl
from jax.experimental.pallas import tpu as pltpu
from jax.sharding import PartitionSpec as P

MESH = pl.DeviceIdType.MESH
BF16 = jnp.bfloat16
F32 = jnp.float32
LANES = 128
RING = 4
EXPERTS = 64
SLOTS = 256
HIDDEN = 768
WIDTH = 4096

ORDERS = ((2, 1, 0), (0, 2, 1), (1, 0, 2))
STARTS = (0, 1408, 2816)
WIDTHS = (1408, 1408, 1280)
TOP = 768
LOWS = (640, 640, 512)
LOW = 640
CARRIED = TOP + LOW
CUTS = ((512, 896), (768, 640), (896, 512))
ENDS = ((256, 512), (384, 384))
PARTS = range(3)


def device_at(place, core):
    x, y, z = place
    return (x * 4 + (z % 2) * 2 + core, (z // 2) * 4 + y)


def expert_at(place, core):
    x, y, z = place
    return x * 16 + (z % 2) * 8 + core * 4 + (z // 2) * 2 + y // 2


def moved(place, axis, value):
    return tuple(value if i == axis else place[i] for i in range(3))


def piece_width(kind, part, piece):
    return CUTS[kind][0] if piece == 0 else WIDTHS[part] - CUTS[kind][0]


def iota(shape, axis):
    return lax.broadcasted_iota(jnp.int32, shape, axis)


def dot(a, b):
    return jnp.dot(a, b, preferred_element_type=F32)


def dot_nt(a, b):
    return lax.dot_general(a, b, (((1,), (1,)), ((), ())), preferred_element_type=F32)


def blocks(width, size):
    return [(i, min(size, width - i)) for i in range(0, width, size)]


def slot_coordinates(index, part):
    first, middle, last = ORDERS[part]
    coords = [None] * 3
    coords[last] = index // 64
    coords[middle] = (index // 8) % 4
    coords[first] = (index // 2) % 4
    return coords, (index // 32) % 2, index % 2


def index_in(part, coords, core, slot):
    first, middle, last = ORDERS[part]
    return coords[last] * 64 + core * 32 + coords[middle] * 8 + coords[first] * 2 + slot


def reorder(part, back):
    rows, cols = iota((SLOTS, SLOTS), 0), iota((SLOTS, SLOTS), 1)
    mine, other = (cols, rows) if back else (rows, cols)
    coords, core, slot = slot_coordinates(mine, part)
    return (index_in(0, coords, core, slot) == other).astype(F32).astype(BF16)


def kernel(
    tokens_hbm, cotangent_hbm, ids_hbm, gates_hbm, gate_hbm, up_hbm, down_hbm,
    mixed_ref, gate_grads_ref, token_grads_ref,
    tokens_ref, cotangent_ref, ids_ref, gates_ref, gate_w, up_w, down_w,
    token_rows, grad_rows, token_send, token_recv, grad_send, grad_recv,
    act, out_send, out_recv, in_send, in_recv,
    out_mid, out_mid_recv, in_mid, in_mid_recv, end_send, end_recv,
    input_sem, weight_sem,
    s1_send, s1_recv, s2_send, s2_recv, t3_send, t3_recv, c3_send, c3_recv,
    m3_send, m3_recv, g3_send, g3_recv, m2_send, m2_recv, g2_send, g2_recv, e1_send, e1_recv,
):
    ctx, dp = lax.axis_index("ctx"), lax.axis_index("dp")
    place = (ctx // 4, dp % 4, (dp // 4) * 2 + (ctx // 2) % 2)
    core = ctx % 2
    expert = expert_at(place, core)

    barrier = pltpu.get_barrier_semaphore()
    peers = [(place, 1 - core)]
    for axis in range(3):
        for offset in range(1, RING):
            there = moved(place, axis, (place[axis] + offset) % RING)
            peers += [(there, core), (there, 1 - core)]
    for there, its_core in peers:
        pl.semaphore_signal(
            barrier, inc=1, device_id=device_at(there, its_core), device_id_type=MESH
        )

    inputs = [
        pltpu.make_async_copy(src, dst, input_sem.at[i])
        for i, (src, dst) in enumerate(
            (
                (ids_hbm, ids_ref),
                (gates_hbm, gates_ref),
                (tokens_hbm, tokens_ref),
                (cotangent_hbm, cotangent_ref),
            )
        )
    ]
    for load in inputs:
        load.start()
    loads = [
        pltpu.make_async_copy(src.at[0], dst, weight_sem.at[i])
        for i, (src, dst) in enumerate(((gate_hbm, gate_w), (up_hbm, up_w), (down_hbm, down_w)))
    ]

    inputs[0].wait()
    inputs[1].wait()
    lane = iota((8, LANES), 1)
    named = jnp.zeros((8, LANES), F32)
    gate = jnp.zeros((8, LANES), F32)
    for k in range(8):
        hit = ids_ref[:, k : k + 1] == lane % EXPERTS
        named = jnp.where(hit, 1.0, named)
        gate = jnp.where(hit, gates_ref[:, k : k + 1], gate)
    row = iota((8, LANES), 0)
    before = jnp.zeros((8, LANES), F32)
    for i in range(7):
        before = before + jnp.where(row > i, named[i : i + 1, :], 0.0)
    slots = jnp.where(before == (lane // EXPERTS).astype(F32), named, 0.0)
    gate_high = gate.astype(BF16).astype(F32)
    gate_tile = jnp.where(lane < EXPERTS, gate_high, gate - gate_high)

    def stacked(ref, p, tiles):
        cut = STARTS[p] + TOP
        top = ref[:, STARTS[p] : cut].astype(F32)
        low = ref[:, cut : cut + LOWS[p]].astype(F32)
        return jnp.concatenate((top, jnp.concatenate((low, *tiles), axis=1)), axis=0).astype(BF16)

    inputs[2].wait()
    for p in PARTS:
        first, middle, last = ORDERS[p]
        tiles = (gate_tile, slots) if p == 2 else (slots,)
        token_rows[p, place[middle], place[first]] = stacked(tokens_ref, p, tiles)
    inputs[3].wait()
    for p in PARTS:
        first, middle, last = ORDERS[p]
        blank = jnp.zeros((8, TOP - LOWS[p]), F32)
        grad_rows[p, place[middle], place[first]] = stacked(cotangent_ref, p, (blank,))

    pl.semaphore_wait(barrier, len(peers))

    def taken(ref, sem):
        pltpu.make_async_copy(ref, ref, sem).wait()

    def ring(axis, source, target, send_sem, recv_sem):
        for offset in (2, 1, 3):
            there = moved(place, axis, (place[axis] + offset) % RING)
            pltpu.make_async_remote_copy(
                src_ref=source(there[axis]),
                dst_ref=target(offset),
                send_sem=send_sem,
                recv_sem=recv_sem,
                device_id=device_at(there, core),
                device_id_type=MESH,
            ).start()

    def exchange(axis, source, target, send_sem, recv_sem):
        mine = target.at[2 * place[axis] + core]
        for offset in (2, 1, 3, 0):
            there = moved(place, axis, (place[axis] + offset) % RING)
            for flip in range(2):
                its_core = core if flip == 0 else 1 - core
                block = source.at[2 * there[axis] + its_core]
                if offset == 0 and flip == 0:
                    pltpu.make_async_copy(block, mine, recv_sem).start()
                    continue
                pltpu.make_async_remote_copy(
                    src_ref=block,
                    dst_ref=mine,
                    send_sem=send_sem,
                    recv_sem=recv_sem,
                    device_id=device_at(there, its_core),
                    device_id_type=MESH,
                ).start()

    kinds = (token_rows, grad_rows)
    for kind, rows in enumerate(kinds):
        for p in PARTS:
            first, middle, last = ORDERS[p]
            home = rows.at[p, place[middle], place[first]]
            ring(
                first, lambda there: home, lambda offset: home,
                s1_send.at[kind], s1_recv.at[kind, p],
            )
    for kind, rows in enumerate(kinds):
        for p in PARTS:
            first, middle, last = ORDERS[p]
            home = rows.at[p, place[middle]]
            taken(rows.at[p, 0, pl.ds(0, 3)], s1_recv.at[kind, p])
            ring(
                middle, lambda there: home, lambda offset: home,
                s2_send.at[kind], s2_recv.at[kind, p],
            )

    for load in loads:
        load.start()

    r0, r1 = iota((SLOTS, SLOTS), 0), iota((SLOTS, SLOTS), 1)
    same = (r0 // 2) % 16 == r1 // 16
    half_masks = [same & ((r1 // 8) % 2 == h) for h in range(2)]
    u0, u1 = iota((SLOTS // 2, SLOTS), 0), iota((SLOTS // 2, SLOTS), 1)
    same_back = u0 // 8 == (u1 // 2) % 16
    lane = iota((SLOTS, LANES), 1)
    to_home, picks = [], []

    def pick_rows(p, h, rows, out, base, width, skip=0):
        for start, size in blocks(width, 256):
            cols = slice(skip + start, skip + start + size)
            part = rows[p, :, :, :, cols].reshape(SLOTS, size)
            out[:, :, base + start : base + start + size] = (
                dot(picks[p][h], part).astype(BF16).reshape(8, 32, size)
            )

    def pick_piece(p, piece):
        begin = piece * CUTS[2][0]
        end = begin + CUTS[2][piece]
        for half, (low, high) in enumerate(((0, TOP), (TOP, CARRIED))):
            left, right = max(begin, low), min(end, high)
            if left < right:
                pick_rows(
                    p, half, token_rows, token_send[piece].at[p], left - begin, right - left,
                    left - low,
                )

    for p in PARTS:
        first, middle, last = ORDERS[p]
        taken(token_rows.at[p, pl.ds(0, 3)], s2_recv.at[0, p])
        index = iota((SLOTS, LANES), 0)
        wanted = expert_at(moved(place, last, index // 64), (index // 32) % 2)
        pick = (lane == (index % 2) * EXPERTS + wanted).astype(F32).astype(BF16)
        tile = token_rows[p, :, :, :, LOW:TOP].reshape(SLOTS, LANES)
        tile = tile.astype(F32).reshape(16, 2, 8, LANES)[:, 1]
        twice = jnp.concatenate((tile, tile), axis=1).reshape(SLOTS, LANES).astype(BF16)
        chosen = dot_nt(pick, twice)
        picks.append([jnp.where(mask, chosen, 0.0).astype(BF16) for mask in half_masks])
        home = dot_nt(tile.reshape(SLOTS // 2, LANES).astype(BF16), pick)
        to_home.append(jnp.where(same_back, home, 0.0).astype(BF16))
        pick_piece(p, 0)
        exchange(
            last, token_send[0].at[p], token_recv[0].at[p], t3_send.at[0], t3_recv.at[0, p]
        )
    for p in PARTS:
        pick_piece(p, 1)
        exchange(
            ORDERS[p][2], token_send[1].at[p], token_recv[1].at[p],
            t3_send.at[1], t3_recv.at[1, p],
        )
    for p in PARTS:
        taken(grad_rows.at[p, pl.ds(0, 3)], s2_recv.at[1, p])
        pick_rows(p, 0, grad_rows, grad_send.at[p], 0, TOP)
        pick_rows(p, 1, grad_rows, grad_send.at[p], TOP, LOW)
        exchange(
            ORDERS[p][2], grad_send.at[p], grad_recv.at[p], c3_send.at[0], c3_recv.at[p]
        )

    def in_order(p, rows):
        return rows if p == 0 else dot(reorder(p, True), rows).astype(BF16)

    gate_slot = None
    loads[0].wait()
    loads[1].wait()
    for h in range(2):
        for p in PARTS:
            taken(token_recv[h].at[p], t3_recv.at[h, p])
            rows = in_order(p, token_recv[h][p].reshape(SLOTS, CUTS[2][h]))
            size = piece_width(2, p, h)
            if h == 1 and p == 2:
                tile = rows[:, size:].astype(F32)
                gate_slot = jnp.sum(
                    jnp.where(lane % EXPERTS == expert, tile, 0.0), axis=1, keepdims=True
                )
                rows = rows[:, :size]
            begin = STARTS[p] + h * CUTS[2][0]
            for i, weight in enumerate((gate_w, up_w)):
                for start, width in blocks(HIDDEN, 256):
                    value = dot(rows, weight[begin : begin + size, start : start + width])
                    if h == 0 and p == 0:
                        act[i, :, start : start + width] = value
                    else:
                        act[i, :, start : start + width] += value
    gate_act, second = act[0], act[1]
    squash = jax.nn.sigmoid(gate_act)
    hidden = gate_act * squash * second
    hidden_gated = (gate_slot * hidden).astype(BF16)
    act[2] = hidden
    loads[2].wait()

    def sent_order(p, value):
        return value if p == 0 else dot(reorder(p, False), value).astype(BF16)

    hidden_sent = [sent_order(p, hidden_gated) for p in PARTS]
    for h in range(2):
        for p in PARTS:
            width = piece_width(0, p, h)
            for start, size in blocks(width, 256):
                at = STARTS[p] + h * CUTS[0][0] + start
                out_send[h][p, :, :, start : start + size] = (
                    dot(hidden_sent[p], down_w[:, at : at + size])
                    .astype(BF16)
                    .reshape(8, 32, size)
                )
            if h == 1 and p == 2:
                out_send[h][p, :, :, width:] = jnp.zeros((8, 32, LANES), BF16)
            exchange(
                ORDERS[p][2], out_send[h].at[p], out_recv[h].at[p],
                m3_send.at[h], m3_recv.at[h, p],
            )

    for p in PARTS:
        taken(grad_recv.at[p], c3_recv.at[p])
        rows = in_order(p, grad_recv[p, :, :, : WIDTHS[p]].reshape(SLOTS, WIDTHS[p]))
        feats = slice(STARTS[p], STARTS[p] + WIDTHS[p])
        for start, size in blocks(HIDDEN, 256):
            value = dot_nt(rows, down_w[start : start + size, feats])
            if p == 0:
                act[3, :, start : start + size] = value
            else:
                act[3, :, start : start + size] += value
    backward = act[3]
    gate_act, second = act[0], act[1]
    squash = jax.nn.sigmoid(gate_act)
    gate_grad = jnp.sum(backward * act[2], axis=1, keepdims=True)
    scaled = backward * gate_slot * squash
    grad_gate = (scaled * second * (1.0 + gate_act * (1.0 - squash))).astype(BF16)
    grad_second = (scaled * gate_act).astype(BF16)
    grad_high = gate_grad.astype(BF16).astype(F32)
    grad_tile = jnp.where(
        lane == expert, grad_high, jnp.where(lane == expert + EXPERTS, gate_grad - grad_high, 0.0)
    ).astype(BF16)
    sent_gate = [sent_order(p, grad_gate) for p in PARTS]
    sent_second = [sent_order(p, grad_second) for p in PARTS]

    def send_gradients(h):
        for p in PARTS:
            width = piece_width(1, p, h)
            for start, size in blocks(width, 256):
                at = STARTS[p] + h * CUTS[1][0] + start
                value = dot_nt(sent_gate[p], gate_w[at : at + size, :]) + dot_nt(
                    sent_second[p], up_w[at : at + size, :]
                )
                in_send[h][p, :, :, start : start + size] = value.astype(BF16).reshape(8, 32, size)
            if h == 1 and p == 2:
                in_send[h][p, :, :, width:] = sent_order(p, grad_tile).reshape(8, 32, LANES)
            exchange(
                ORDERS[p][2], in_send[h].at[p], in_recv[h].at[p],
                g3_send.at[h], g3_recv.at[h, p],
            )

    def slot_sum(p, recv, mid, width, sem):
        taken(recv, sem)
        for start, size in blocks(width, 256):
            rows = recv[:, :, start : start + size].reshape(SLOTS, size)
            mid[:, :, start : start + size] = (
                dot(to_home[p], rows).astype(BF16).reshape(RING, 32, size)
            )

    def to_middle(p, mid, mid_recv, send_sem, recv_sem):
        ring(
            ORDERS[p][1], lambda there: mid.at[there], lambda offset: mid_recv.at[offset - 1],
            send_sem, recv_sem,
        )

    def middle_sum(p, mid, mid_recv, sem):
        taken(mid_recv, sem)
        value = mid[place[ORDERS[p][1]]].astype(F32)
        for i in range(3):
            value = value + mid_recv[i].astype(F32)
        return value.reshape(RING, 8, value.shape[-1])

    def end_cols(kind, h):
        return slice(h * ENDS[kind][0], h * ENDS[kind][0] + ENDS[kind][h])

    def end_pack(kind, p, h, value):
        size = ENDS[kind][h]
        rest = value[:, :, size:]
        if rest.shape[2] < size:
            blank = jnp.zeros((RING, 8, size - rest.shape[2]), F32)
            rest = jnp.concatenate((rest, blank), axis=2)
        end_send[kind, p, :, :, end_cols(kind, h)] = jnp.concatenate(
            (value[:, :, :size], rest), axis=1
        ).astype(BF16)

    def to_end(kind, p, cols, send_sem, recv_sem):
        send = end_send.at[kind, p]
        ring(
            ORDERS[p][0], lambda there: send.at[there, :, cols],
            lambda offset: end_recv.at[kind, p, offset - 1, :, cols], send_sem, recv_sem,
        )

    send_gradients(0)
    send_gradients(1)
    for h in range(2):
        for p in PARTS:
            mid = in_mid[h].at[p]
            slot_sum(p, in_recv[h].at[p], mid, CUTS[1][h], g3_recv.at[h, p])
            to_middle(p, mid, in_mid_recv[h].at[p], g2_send.at[h], g2_recv.at[h, p])
        if h == 0:
            for p in PARTS:
                for i in range(2):
                    width = CUTS[0][i]
                    mid = out_mid.at[p, :, :, pl.ds(i * CUTS[0][0], width)]
                    slot_sum(p, out_recv[i].at[p], mid, width, m3_recv.at[i, p])
                to_middle(p, out_mid.at[p], out_mid_recv.at[p], m2_send.at[0], m2_recv.at[p])

    def end_gradients(h):
        for p in PARTS:
            value = middle_sum(p, in_mid[h].at[p], in_mid_recv[h].at[p], g2_recv.at[h, p])
            end_pack(1, p, h, value)
            to_end(1, p, end_cols(1, h), e1_send.at[h], e1_recv.at[h, p])

    end_gradients(0)
    for p in PARTS:
        value = middle_sum(p, out_mid.at[p], out_mid_recv.at[p], m2_recv.at[p])
        end_pack(0, p, 0, value[:, :, : CUTS[0][0]])
        end_pack(0, p, 1, value[:, :, CUTS[0][0] :])
        to_end(0, p, slice(0, TOP), e1_send.at[2], e1_recv.at[2, p])
    end_gradients(1)

    def finish(kind, out_ref, p, h):
        cols = end_cols(kind, h)
        value = end_send[kind, p, place[ORDERS[p][0]], :, cols].astype(F32)
        for i in range(3):
            value = value + end_recv[kind, p, i, :, cols].astype(F32)
        begin = STARTS[p] + h * CUTS[kind][0]
        size = ENDS[kind][h]
        rest = piece_width(kind, p, h) - size
        out_ref[:, begin : begin + size] = value[:8].astype(BF16)
        if rest > 0:
            out_ref[:, begin + size : begin + size + rest] = value[8:, :rest].astype(BF16)
        return value[8:, rest : rest + LANES]

    for p in PARTS:
        taken(end_recv.at[0, p], e1_recv.at[2, p])
        for h in range(2):
            finish(0, mixed_ref, p, h)
    for h in range(2):
        for p in PARTS:
            taken(end_recv.at[1, p, :, :, end_cols(1, h)], e1_recv.at[h, p])
            tile = finish(1, token_grads_ref, p, h)
    lane8 = iota((8, LANES), 1)
    column = iota((8, 8), 1)
    grads = jnp.zeros((8, 8), F32)
    for k in range(8):
        hit = ids_ref[:, k : k + 1] == lane8 % EXPERTS
        picked = jnp.sum(jnp.where(hit, tile, 0.0), axis=1, keepdims=True)
        grads = jnp.where(column == k, picked, grads)
    gate_grads_ref[...] = grads

    for kind, rows in enumerate(kinds):
        taken(rows.at[:, 0, pl.ds(0, 3)], s1_send.at[kind])
        taken(rows.at[:, pl.ds(0, 3)], s2_send.at[kind])
    for h in range(2):
        taken(token_send[h].at[:, pl.ds(0, 7)], t3_send.at[h])
        taken(in_send[h].at[:, pl.ds(0, 7)], g3_send.at[h])
        taken(in_mid[h].at[:, pl.ds(0, 3)], g2_send.at[h])
        taken(out_send[h].at[:, pl.ds(0, 7)], m3_send.at[h])
        taken(end_send.at[1, :, pl.ds(0, 3), :, end_cols(1, h)], e1_send.at[h])
    taken(grad_send.at[:, pl.ds(0, 7)], c3_send.at[0])
    taken(end_send.at[0, :, pl.ds(0, 3)], e1_send.at[2])
    taken(out_mid.at[:, pl.ds(0, 3)], m2_send.at[0])


def hand_over(*refs):
    for source, target in zip(refs[:3], refs[3:]):
        target[...] = source[...]


def shards(tokens, cotangent, expert_ids, gates, gate_weight, up_weight, down_weight):
    def vmem(shape, dtype=BF16):
        return pltpu.VMEM(shape, dtype)

    def parts(shape, widths, dtype=BF16):
        return [vmem((*shape, width), dtype) for width in widths]

    dma = pltpu.SemaphoreType.DMA
    block = (3, 8, 32)
    whole = pl.BlockSpec(memory_space=pltpu.VMEM)
    hbm = pl.BlockSpec(memory_space=pl.ANY)
    out_shape = (
        jax.ShapeDtypeStruct((8, WIDTH), BF16),
        jax.ShapeDtypeStruct((8, 8), F32),
        jax.ShapeDtypeStruct((8, WIDTH), BF16),
    )
    results = pl.pallas_call(
        kernel,
        out_shape=out_shape,
        in_specs=[hbm] * 7,
        out_specs=[whole] * 3,
        scratch_shapes=[
            vmem((8, WIDTH)),
            vmem((8, WIDTH)),
            vmem((8, 8), jnp.int32),
            vmem((8, 8), F32),
            vmem((WIDTH, HIDDEN)),
            vmem((WIDTH, HIDDEN)),
            vmem((HIDDEN, WIDTH)),
            vmem((3, RING, RING, 16, TOP)),
            vmem((3, RING, RING, 16, TOP)),
            parts(block, CUTS[2]),
            parts(block, CUTS[2]),
            vmem((*block, CARRIED)),
            vmem((*block, CARRIED)),
            vmem((4, SLOTS, HIDDEN), F32),
            parts(block, CUTS[0]),
            parts(block, CUTS[0]),
            parts(block, CUTS[1]),
            parts(block, CUTS[1]),
            vmem((3, RING, 32, CARRIED)),
            vmem((3, RING - 1, 32, CARRIED)),
            parts((3, RING, 32), CUTS[1]),
            parts((3, RING - 1, 32), CUTS[1]),
            vmem((2, 3, RING, 16, TOP)),
            vmem((2, 3, RING - 1, 16, TOP)),
            dma((4,)),
            dma((3,)),
            dma((2,)), dma((2, 3)), dma((2,)), dma((2, 3)),
            dma((2,)), dma((2, 3)), dma((1,)), dma((3,)),
            dma((2,)), dma((2, 3)), dma((2,)), dma((2, 3)),
            dma((1,)), dma((3,)), dma((2,)), dma((2, 3)),
            dma((3,)), dma((3, 3)),
        ],
        compiler_params=pltpu.CompilerParams(
            collective_id=0, has_side_effects=True, vmem_limit_bytes=60 * 2**20
        ),
    )(tokens, cotangent, expert_ids, gates, gate_weight, up_weight, down_weight)
    return pl.pallas_call(
        hand_over,
        out_shape=out_shape,
        in_specs=[whole] * 3,
        out_specs=[whole] * 3,
    )(*results)


def solution(mesh):
    rows = P(("ctx", "dp"), None)
    weights = P(("ctx", "dp"), None, None)
    return jax.shard_map(
        shards,
        mesh=mesh,
        in_specs=(rows, rows, rows, rows, weights, weights, weights),
        out_specs=(rows, rows, rows),
        check_vma=False,
    )
```

```python
import functools

import jax
import jax.numpy as jnp
from jax import lax
from jax.experimental import pallas as pl
from jax.experimental.pallas import tpu as pltpu
from jax.sharding import PartitionSpec as P

MESH = pl.DeviceIdType.MESH
BF16 = jnp.bfloat16
F32 = jnp.float32
LANES = 128
RING = 4
EXPERTS = 64
SLOTS = 256
HIDDEN = 768
WIDTH = 4096

ORDERS = ((2, 1, 0), (0, 2, 1), (1, 0, 2))
STARTS = (0, 1408, 2816)
WIDTHS = (1408, 1408, 1280)
TOP = 768
LOWS = (640, 640, 512)
LOW = 640
CARRIED = TOP + LOW
CUTS = ((512, 896), (768, 640), (896, 512))
ENDS = ((256, 512), (384, 384))
PARTS = range(3)


def device_at(place, core):
    x, y, z = place
    return (x * 4 + (z % 2) * 2 + core, (z // 2) * 4 + y)


def expert_at(place, core):
    x, y, z = place
    return x * 16 + (z % 2) * 8 + core * 4 + (z // 2) * 2 + y // 2


def moved(place, axis, value):
    return tuple(value if i == axis else place[i] for i in range(3))


def piece_width(kind, part, piece):
    return CUTS[kind][0] if piece == 0 else WIDTHS[part] - CUTS[kind][0]


def iota(shape, axis):
    return lax.broadcasted_iota(jnp.int32, shape, axis)


def dot(a, b):
    return jnp.dot(a, b, preferred_element_type=F32)


def dot_nt(a, b):
    return lax.dot_general(a, b, (((1,), (1,)), ((), ())), preferred_element_type=F32)


def blocks(width, size):
    return [(i, min(size, width - i)) for i in range(0, width, size)]


def slot_coordinates(index, part):
    first, middle, last = ORDERS[part]
    coords = [None] * 3
    coords[last] = index // 64
    coords[middle] = (index // 8) % 4
    coords[first] = (index // 2) % 4
    return coords, (index // 32) % 2, index % 2


def index_in(part, coords, core, slot):
    first, middle, last = ORDERS[part]
    return coords[last] * 64 + core * 32 + coords[middle] * 8 + coords[first] * 2 + slot


def reorder(part, back):
    rows, cols = iota((SLOTS, SLOTS), 0), iota((SLOTS, SLOTS), 1)
    mine, other = (cols, rows) if back else (rows, cols)
    coords, core, slot = slot_coordinates(mine, part)
    return (index_in(0, coords, core, slot) == other).astype(F32).astype(BF16)


def kernel(
    tokens_hbm, cotangent_hbm, ids_hbm, gates_hbm, gate_hbm, up_hbm, down_hbm,
    mixed_ref, gate_grads_ref, token_grads_ref,
    tokens_ref, cotangent_ref, ids_ref, gates_ref, gate_w, up_w, down_w,
    token_rows, grad_rows, token_send, token_recv, grad_send, grad_recv,
    act, out_send, out_recv, in_send, in_recv,
    out_mid, out_mid_recv, in_mid, in_mid_recv, end_send, end_recv,
    input_sem, weight_sem,
    s1_send, s1_recv, s2_send, s2_recv, t3_send, t3_recv, c3_send, c3_recv,
    m3_send, m3_recv, g3_send, g3_recv, m2_send, m2_recv, g2_send, g2_recv, e1_send, e1_recv,
):
    ctx, dp = lax.axis_index("ctx"), lax.axis_index("dp")
    place = (ctx // 4, dp % 4, (dp // 4) * 2 + (ctx // 2) % 2)
    core = ctx % 2
    expert = expert_at(place, core)

    barrier = pltpu.get_barrier_semaphore()
    peers = [(place, 1 - core)]
    for axis in range(3):
        for offset in range(1, RING):
            there = moved(place, axis, (place[axis] + offset) % RING)
            peers += [(there, core), (there, 1 - core)]
    for there, its_core in peers:
        pl.semaphore_signal(
            barrier, inc=1, device_id=device_at(there, its_core), device_id_type=MESH
        )

    inputs = [
        pltpu.make_async_copy(src, dst, input_sem.at[i])
        for i, (src, dst) in enumerate(
            (
                (ids_hbm, ids_ref),
                (gates_hbm, gates_ref),
                (tokens_hbm, tokens_ref),
                (cotangent_hbm, cotangent_ref),
            )
        )
    ]
    for load in inputs:
        load.start()
    loads = [
        pltpu.make_async_copy(src.at[0], dst, weight_sem.at[i])
        for i, (src, dst) in enumerate(((gate_hbm, gate_w), (up_hbm, up_w), (down_hbm, down_w)))
    ]

    inputs[0].wait()
    inputs[1].wait()
    lane = iota((8, LANES), 1)
    named = jnp.zeros((8, LANES), F32)
    gate = jnp.zeros((8, LANES), F32)
    for k in range(8):
        hit = ids_ref[:, k : k + 1] == lane % EXPERTS
        named = jnp.where(hit, 1.0, named)
        gate = jnp.where(hit, gates_ref[:, k : k + 1], gate)
    row = iota((8, LANES), 0)
    before = jnp.zeros((8, LANES), F32)
    for i in range(7):
        before = before + jnp.where(row > i, named[i : i + 1, :], 0.0)
    slots = jnp.where(before == (lane // EXPERTS).astype(F32), named, 0.0)
    gate_high = gate.astype(BF16).astype(F32)
    gate_tile = jnp.where(lane < EXPERTS, gate_high, gate - gate_high)

    def stacked(ref, p, tiles):
        cut = STARTS[p] + TOP
        top = ref[:, STARTS[p] : cut].astype(F32)
        low = ref[:, cut : cut + LOWS[p]].astype(F32)
        return jnp.concatenate((top, jnp.concatenate((low, *tiles), axis=1)), axis=0).astype(BF16)

    inputs[2].wait()
    for p in PARTS:
        first, middle, last = ORDERS[p]
        tiles = (gate_tile, slots) if p == 2 else (slots,)
        token_rows[p, place[middle], place[first]] = stacked(tokens_ref, p, tiles)
    inputs[3].wait()
    for p in PARTS:
        first, middle, last = ORDERS[p]
        blank = jnp.zeros((8, TOP - LOWS[p]), F32)
        grad_rows[p, place[middle], place[first]] = stacked(cotangent_ref, p, (blank,))

    pl.semaphore_wait(barrier, len(peers))

    def taken(ref, sem):
        pltpu.make_async_copy(ref, ref, sem).wait()

    def ring(axis, source, target, send_sem, recv_sem):
        for offset in (2, 1, 3):
            there = moved(place, axis, (place[axis] + offset) % RING)
            pltpu.make_async_remote_copy(
                src_ref=source(there[axis]),
                dst_ref=target(offset),
                send_sem=send_sem,
                recv_sem=recv_sem,
                device_id=device_at(there, core),
                device_id_type=MESH,
            ).start()

    def exchange(axis, source, target, send_sem, recv_sem):
        mine = target.at[2 * place[axis] + core]
        for offset in (2, 1, 3, 0):
            there = moved(place, axis, (place[axis] + offset) % RING)
            for flip in range(2):
                its_core = core if flip == 0 else 1 - core
                block = source.at[2 * there[axis] + its_core]
                if offset == 0 and flip == 0:
                    pltpu.make_async_copy(block, mine, recv_sem).start()
                    continue
                pltpu.make_async_remote_copy(
                    src_ref=block,
                    dst_ref=mine,
                    send_sem=send_sem,
                    recv_sem=recv_sem,
                    device_id=device_at(there, its_core),
                    device_id_type=MESH,
                ).start()

    kinds = (token_rows, grad_rows)
    for kind, rows in enumerate(kinds):
        for p in PARTS:
            first, middle, last = ORDERS[p]
            home = rows.at[p, place[middle], place[first]]
            ring(
                first, lambda there: home, lambda offset: home,
                s1_send.at[kind], s1_recv.at[kind, p],
            )
    for kind, rows in enumerate(kinds):
        for p in PARTS:
            first, middle, last = ORDERS[p]
            home = rows.at[p, place[middle]]
            taken(rows.at[p, 0, pl.ds(0, 3)], s1_recv.at[kind, p])
            ring(
                middle, lambda there: home, lambda offset: home,
                s2_send.at[kind], s2_recv.at[kind, p],
            )

    loads[0].start()
    loads[1].start()

    r0, r1 = iota((SLOTS, SLOTS), 0), iota((SLOTS, SLOTS), 1)
    same = (r0 // 2) % 16 == r1 // 16
    half_masks = [same & ((r1 // 8) % 2 == h) for h in range(2)]
    u0, u1 = iota((SLOTS // 2, SLOTS), 0), iota((SLOTS // 2, SLOTS), 1)
    same_back = u0 // 8 == (u1 // 2) % 16
    lane = iota((SLOTS, LANES), 1)
    to_home, picks = [], []

    def pick_rows(p, h, rows, out, base, width, skip=0):
        for start, size in blocks(width, 256):
            cols = slice(skip + start, skip + start + size)
            part = rows[p, :, :, :, cols].reshape(SLOTS, size)
            out[:, :, base + start : base + start + size] = (
                dot(picks[p][h], part).astype(BF16).reshape(8, 32, size)
            )

    def pick_piece(p, piece):
        begin = piece * CUTS[2][0]
        end = begin + CUTS[2][piece]
        for half, (low, high) in enumerate(((0, TOP), (TOP, CARRIED))):
            left, right = max(begin, low), min(end, high)
            if left < right:
                pick_rows(
                    p, half, token_rows, token_send[piece].at[p], left - begin, right - left,
                    left - low,
                )

    for p in PARTS:
        first, middle, last = ORDERS[p]
        taken(token_rows.at[p, pl.ds(0, 3)], s2_recv.at[0, p])
        index = iota((SLOTS, LANES), 0)
        wanted = expert_at(moved(place, last, index // 64), (index // 32) % 2)
        pick = (lane == (index % 2) * EXPERTS + wanted).astype(F32).astype(BF16)
        tile = token_rows[p, :, :, :, LOW:TOP].reshape(SLOTS, LANES)
        tile = tile.astype(F32).reshape(16, 2, 8, LANES)[:, 1]
        twice = jnp.concatenate((tile, tile), axis=1).reshape(SLOTS, LANES).astype(BF16)
        chosen = dot_nt(pick, twice)
        picks.append([jnp.where(mask, chosen, 0.0).astype(BF16) for mask in half_masks])
        home = dot_nt(tile.reshape(SLOTS // 2, LANES).astype(BF16), pick)
        to_home.append(jnp.where(same_back, home, 0.0).astype(BF16))
        pick_piece(p, 0)
        exchange(
            last, token_send[0].at[p], token_recv[0].at[p], t3_send.at[0], t3_recv.at[0, p]
        )
    for p in PARTS:
        pick_piece(p, 1)
        exchange(
            ORDERS[p][2], token_send[1].at[p], token_recv[1].at[p],
            t3_send.at[1], t3_recv.at[1, p],
        )
    for p in PARTS:
        taken(grad_rows.at[p, pl.ds(0, 3)], s2_recv.at[1, p])
        pick_rows(p, 0, grad_rows, grad_send.at[p], 0, TOP)
        pick_rows(p, 1, grad_rows, grad_send.at[p], TOP, LOW)
        exchange(
            ORDERS[p][2], grad_send.at[p], grad_recv.at[p], c3_send.at[0], c3_recv.at[p]
        )

    loads[2].start()

    def in_order(p, rows):
        return rows if p == 0 else dot(reorder(p, True), rows).astype(BF16)

    gate_slot = None
    loads[0].wait()
    loads[1].wait()
    for h in range(2):
        for p in PARTS:
            taken(token_recv[h].at[p], t3_recv.at[h, p])
            rows = in_order(p, token_recv[h][p].reshape(SLOTS, CUTS[2][h]))
            size = piece_width(2, p, h)
            if h == 1 and p == 2:
                tile = rows[:, size:].astype(F32)
                gate_slot = jnp.sum(
                    jnp.where(lane % EXPERTS == expert, tile, 0.0), axis=1, keepdims=True
                )
                rows = rows[:, :size]
            begin = STARTS[p] + h * CUTS[2][0]
            for i, weight in enumerate((gate_w, up_w)):
                for start, width in blocks(HIDDEN, 256):
                    value = dot(rows, weight[begin : begin + size, start : start + width])
                    if h == 0 and p == 0:
                        act[i, :, start : start + width] = value
                    else:
                        act[i, :, start : start + width] += value
    gate_act, second = act[0], act[1]
    squash = jax.nn.sigmoid(gate_act)
    hidden = gate_act * squash * second
    hidden_gated = (gate_slot * hidden).astype(BF16)
    act[2] = hidden
    loads[2].wait()

    def sent_order(p, value):
        return value if p == 0 else dot(reorder(p, False), value).astype(BF16)

    hidden_sent = [sent_order(p, hidden_gated) for p in PARTS]
    for h in range(2):
        for p in PARTS:
            width = piece_width(0, p, h)
            for start, size in blocks(width, 256):
                at = STARTS[p] + h * CUTS[0][0] + start
                out_send[h][p, :, :, start : start + size] = (
                    dot(hidden_sent[p], down_w[:, at : at + size])
                    .astype(BF16)
                    .reshape(8, 32, size)
                )
            if h == 1 and p == 2:
                out_send[h][p, :, :, width:] = jnp.zeros((8, 32, LANES), BF16)
            exchange(
                ORDERS[p][2], out_send[h].at[p], out_recv[h].at[p],
                m3_send.at[h], m3_recv.at[h, p],
            )

    for p in PARTS:
        taken(grad_recv.at[p], c3_recv.at[p])
        rows = in_order(p, grad_recv[p, :, :, : WIDTHS[p]].reshape(SLOTS, WIDTHS[p]))
        feats = slice(STARTS[p], STARTS[p] + WIDTHS[p])
        for start, size in blocks(HIDDEN, 256):
            value = dot_nt(rows, down_w[start : start + size, feats])
            if p == 0:
                act[3, :, start : start + size] = value
            else:
                act[3, :, start : start + size] += value
    backward = act[3]
    gate_act, second = act[0], act[1]
    squash = jax.nn.sigmoid(gate_act)
    gate_grad = jnp.sum(backward * act[2], axis=1, keepdims=True)
    scaled = backward * gate_slot * squash
    grad_gate = (scaled * second * (1.0 + gate_act * (1.0 - squash))).astype(BF16)
    grad_second = (scaled * gate_act).astype(BF16)
    grad_high = gate_grad.astype(BF16).astype(F32)
    grad_tile = jnp.where(
        lane == expert, grad_high, jnp.where(lane == expert + EXPERTS, gate_grad - grad_high, 0.0)
    ).astype(BF16)
    sent_gate = [sent_order(p, grad_gate) for p in PARTS]
    sent_second = [sent_order(p, grad_second) for p in PARTS]

    def send_gradients(h):
        for p in PARTS:
            width = piece_width(1, p, h)
            for start, size in blocks(width, 256):
                at = STARTS[p] + h * CUTS[1][0] + start
                value = dot_nt(sent_gate[p], gate_w[at : at + size, :]) + dot_nt(
                    sent_second[p], up_w[at : at + size, :]
                )
                in_send[h][p, :, :, start : start + size] = value.astype(BF16).reshape(8, 32, size)
            if h == 1 and p == 2:
                in_send[h][p, :, :, width:] = sent_order(p, grad_tile).reshape(8, 32, LANES)
            exchange(
                ORDERS[p][2], in_send[h].at[p], in_recv[h].at[p],
                g3_send.at[h], g3_recv.at[h, p],
            )

    def slot_sum(p, recv, mid, width, sem):
        taken(recv, sem)
        for start, size in blocks(width, 256):
            rows = recv[:, :, start : start + size].reshape(SLOTS, size)
            mid[:, :, start : start + size] = (
                dot(to_home[p], rows).astype(BF16).reshape(RING, 32, size)
            )

    def to_middle(p, mid, mid_recv, send_sem, recv_sem):
        ring(
            ORDERS[p][1], lambda there: mid.at[there], lambda offset: mid_recv.at[offset - 1],
            send_sem, recv_sem,
        )

    def middle_sum(p, mid, mid_recv, sem):
        taken(mid_recv, sem)
        value = mid[place[ORDERS[p][1]]].astype(F32)
        for i in range(3):
            value = value + mid_recv[i].astype(F32)
        return value.reshape(RING, 8, value.shape[-1])

    def end_cols(kind, h):
        return slice(h * ENDS[kind][0], h * ENDS[kind][0] + ENDS[kind][h])

    def end_pack(kind, p, h, value):
        size = ENDS[kind][h]
        rest = value[:, :, size:]
        if rest.shape[2] < size:
            blank = jnp.zeros((RING, 8, size - rest.shape[2]), F32)
            rest = jnp.concatenate((rest, blank), axis=2)
        end_send[kind, p, :, :, end_cols(kind, h)] = jnp.concatenate(
            (value[:, :, :size], rest), axis=1
        ).astype(BF16)

    def to_end(kind, p, cols, send_sem, recv_sem):
        send = end_send.at[kind, p]
        ring(
            ORDERS[p][0], lambda there: send.at[there, :, cols],
            lambda offset: end_recv.at[kind, p, offset - 1, :, cols], send_sem, recv_sem,
        )

    send_gradients(0)
    send_gradients(1)
    for h in range(2):
        for p in PARTS:
            mid = in_mid[h].at[p]
            slot_sum(p, in_recv[h].at[p], mid, CUTS[1][h], g3_recv.at[h, p])
            to_middle(p, mid, in_mid_recv[h].at[p], g2_send.at[h], g2_recv.at[h, p])
        if h == 0:
            for p in PARTS:
                for i in range(2):
                    width = CUTS[0][i]
                    mid = out_mid.at[p, :, :, pl.ds(i * CUTS[0][0], width)]
                    slot_sum(p, out_recv[i].at[p], mid, width, m3_recv.at[i, p])
                to_middle(p, out_mid.at[p], out_mid_recv.at[p], m2_send.at[0], m2_recv.at[p])

    def end_gradients(h):
        for p in PARTS:
            value = middle_sum(p, in_mid[h].at[p], in_mid_recv[h].at[p], g2_recv.at[h, p])
            end_pack(1, p, h, value)
            to_end(1, p, end_cols(1, h), e1_send.at[h], e1_recv.at[h, p])

    end_gradients(0)
    for p in PARTS:
        value = middle_sum(p, out_mid.at[p], out_mid_recv.at[p], m2_recv.at[p])
        end_pack(0, p, 0, value[:, :, : CUTS[0][0]])
        end_pack(0, p, 1, value[:, :, CUTS[0][0] :])
        to_end(0, p, slice(0, TOP), e1_send.at[2], e1_recv.at[2, p])
    end_gradients(1)

    def finish(kind, out_ref, p, h):
        cols = end_cols(kind, h)
        value = end_send[kind, p, place[ORDERS[p][0]], :, cols].astype(F32)
        for i in range(3):
            value = value + end_recv[kind, p, i, :, cols].astype(F32)
        begin = STARTS[p] + h * CUTS[kind][0]
        size = ENDS[kind][h]
        rest = piece_width(kind, p, h) - size
        out_ref[:, begin : begin + size] = value[:8].astype(BF16)
        if rest > 0:
            out_ref[:, begin + size : begin + size + rest] = value[8:, :rest].astype(BF16)
        return value[8:, rest : rest + LANES]

    for p in PARTS:
        taken(end_recv.at[0, p], e1_recv.at[2, p])
        for h in range(2):
            finish(0, mixed_ref, p, h)
    for h in range(2):
        for p in PARTS:
            taken(end_recv.at[1, p, :, :, end_cols(1, h)], e1_recv.at[h, p])
            tile = finish(1, token_grads_ref, p, h)
    lane8 = iota((8, LANES), 1)
    column = iota((8, 8), 1)
    grads = jnp.zeros((8, 8), F32)
    for k in range(8):
        hit = ids_ref[:, k : k + 1] == lane8 % EXPERTS
        picked = jnp.sum(jnp.where(hit, tile, 0.0), axis=1, keepdims=True)
        grads = jnp.where(column == k, picked, grads)
    gate_grads_ref[...] = grads

    for kind, rows in enumerate(kinds):
        taken(rows.at[:, 0, pl.ds(0, 3)], s1_send.at[kind])
        taken(rows.at[:, pl.ds(0, 3)], s2_send.at[kind])
    for h in range(2):
        taken(token_send[h].at[:, pl.ds(0, 7)], t3_send.at[h])
        taken(in_send[h].at[:, pl.ds(0, 7)], g3_send.at[h])
        taken(in_mid[h].at[:, pl.ds(0, 3)], g2_send.at[h])
        taken(out_send[h].at[:, pl.ds(0, 7)], m3_send.at[h])
        taken(end_send.at[1, :, pl.ds(0, 3), :, end_cols(1, h)], e1_send.at[h])
    taken(grad_send.at[:, pl.ds(0, 7)], c3_send.at[0])
    taken(end_send.at[0, :, pl.ds(0, 3)], e1_send.at[2])
    taken(out_mid.at[:, pl.ds(0, 3)], m2_send.at[0])


def hand_over(*refs):
    for source, target in zip(refs[:3], refs[3:]):
        target[...] = source[...]


def shards(tokens, cotangent, expert_ids, gates, gate_weight, up_weight, down_weight):
    def vmem(shape, dtype=BF16):
        return pltpu.VMEM(shape, dtype)

    def parts(shape, widths, dtype=BF16):
        return [vmem((*shape, width), dtype) for width in widths]

    dma = pltpu.SemaphoreType.DMA
    block = (3, 8, 32)
    whole = pl.BlockSpec(memory_space=pltpu.VMEM)
    hbm = pl.BlockSpec(memory_space=pl.ANY)
    out_shape = (
        jax.ShapeDtypeStruct((8, WIDTH), BF16),
        jax.ShapeDtypeStruct((8, 8), F32),
        jax.ShapeDtypeStruct((8, WIDTH), BF16),
    )
    results = pl.pallas_call(
        kernel,
        out_shape=out_shape,
        in_specs=[hbm] * 7,
        out_specs=[whole] * 3,
        scratch_shapes=[
            vmem((8, WIDTH)),
            vmem((8, WIDTH)),
            vmem((8, 8), jnp.int32),
            vmem((8, 8), F32),
            vmem((WIDTH, HIDDEN)),
            vmem((WIDTH, HIDDEN)),
            vmem((HIDDEN, WIDTH)),
            vmem((3, RING, RING, 16, TOP)),
            vmem((3, RING, RING, 16, TOP)),
            parts(block, CUTS[2]),
            parts(block, CUTS[2]),
            vmem((*block, CARRIED)),
            vmem((*block, CARRIED)),
            vmem((4, SLOTS, HIDDEN), F32),
            parts(block, CUTS[0]),
            parts(block, CUTS[0]),
            parts(block, CUTS[1]),
            parts(block, CUTS[1]),
            vmem((3, RING, 32, CARRIED)),
            vmem((3, RING - 1, 32, CARRIED)),
            parts((3, RING, 32), CUTS[1]),
            parts((3, RING - 1, 32), CUTS[1]),
            vmem((2, 3, RING, 16, TOP)),
            vmem((2, 3, RING - 1, 16, TOP)),
            dma((4,)),
            dma((3,)),
            dma((2,)), dma((2, 3)), dma((2,)), dma((2, 3)),
            dma((2,)), dma((2, 3)), dma((1,)), dma((3,)),
            dma((2,)), dma((2, 3)), dma((2,)), dma((2, 3)),
            dma((1,)), dma((3,)), dma((2,)), dma((2, 3)),
            dma((3,)), dma((3, 3)),
        ],
        compiler_params=pltpu.CompilerParams(
            collective_id=0, has_side_effects=True, vmem_limit_bytes=60 * 2**20
        ),
    )(tokens, cotangent, expert_ids, gates, gate_weight, up_weight, down_weight)
    return pl.pallas_call(
        hand_over,
        out_shape=out_shape,
        in_specs=[whole] * 3,
        out_specs=[whole] * 3,
    )(*results)


def solution(mesh):
    rows = P(("ctx", "dp"), None)
    weights = P(("ctx", "dp"), None, None)
    return jax.shard_map(
        shards,
        mesh=mesh,
        in_specs=(rows, rows, rows, rows, weights, weights, weights),
        out_specs=(rows, rows, rows),
        check_vma=False,
    )
```
